32 devices in a mesh: group: 4 (over y, x), sample: 8 (over z, core).
Axes of the slice: x: 2, y: 2, z: 4, core: 2. Of those that a mesh axis runs over, the one named last changes fastest.
Arguments:
- response_rows: bfloat16 [4096, 4096], P(('group', 'sample')), may hold values from -6 to 6
- prompt_rows: bfloat16 [2048, 4096], P(('group', 'sample')), may hold values from -6 to 6
- queries: bfloat16 [4096, 4096], P(('group', 'sample')), may hold values from -4.5 to 4.5
- response_keys: bfloat16 [4096, 512], P(('group', 'sample')), may hold values from -6 to 6
- prompt_keys: bfloat16 [2048, 512], P(('group', 'sample')), may hold values from -5 to 5
- cotangent: bfloat16 [4096, 4096], P(('group', 'sample')), may hold values from -96 to 96
- segment_index: int32 [32, 128], P(('group', 'sample')), may hold values from 0 to 7, never falling along the last dimension, each value on 1 to 32 neighbouring positions
- prompt_choice: int32 [32, 8], P(('group', 'sample')), may hold values from 0 to 3
- frozen_value_weight: bfloat16 [4096, 512], P('sample'), may hold values from -0.09375 to 0.09375
- value_adapter_down: bfloat16 [4096, 16], P('sample'), may hold values from -0.09375 to 0.09375
- value_adapter_up: bfloat16 [16, 512], replicated, may hold values from -1.5 to 1.5
Outputs:
- response_grad: bfloat16 [4096, 4096], P(('group', 'sample'))
- prompt_grad: bfloat16 [2048, 4096], P(('group', 'sample'))
- response_key_grad: bfloat16 [4096, 512], P(('group', 'sample'))
- prompt_key_grad: bfloat16 [2048, 512], P(('group', 'sample'))
- first_grad: float32 [4096, 16], P('sample')
- second_grad: float32 [16, 512], replicated
The draws below stay inside these ranges and needn't reach their ends.
Inputs may be any that keep to these rules, and one draw needn't show every extreme that they name: `segment_index`: within the 128 tokens of one device the response number never falls; each of the 8 responses has 1 to 32 tokens, and one has exactly 32.
All inputs are finite; a program needn't handle non-finite values.
Results may differ from the reference program's by a relative error of at most 0.015.
Values may be sent and summed in bfloat16 or wider, within the bound.
A program may use at most 128 MiB of HBM per device.

```python
import math
import jax
import jax.numpy as jnp
import numpy as np
from jax import lax

D = 4096
HEADS = 32
KV_HEADS = 4
HEAD_DIM = 128
RANK = 16
PROMPTS = 4
PROMPT_LEN = 128
RESP_DEV = 128
RESPONSES = 8
RESP_MOST = 32
RESP_TOK = 4096
PROMPT_ROWS = 2048
TOKEN_TOTAL = 6144
N_GROUP = 4
N_SAMPLE = 8


def draw_queries(key, part):
    key = jax.random.fold_in(key, 7)
    first_key = jax.random.fold_in(key, 0)
    shape = (RESP_TOK, HEADS * HEAD_DIM)
    base = jnp.clip(jax.random.normal(first_key, shape, jnp.float32), -4.5, 4.5)
    return base.astype(jnp.bfloat16)


def draw_prompt_keys(key, part):
    key = jax.random.fold_in(key, 11)
    shape = (PROMPT_ROWS, KV_HEADS * HEAD_DIM)
    base = jnp.clip(jax.random.normal(key, shape, jnp.float32), -5.0, 5.0)
    return base.astype(jnp.bfloat16)


def touch_ends(result, own_key, least, high):
    longest = result.shape.index(max(result.shape))
    spots = []
    for shift in (0, 1):
        where = [jax.random.randint(jax.random.fold_in(own_key, axis), (), 0, length) for axis, length in enumerate(result.shape)]
        where[longest] = (where[longest] + shift) % result.shape[longest]
        spots.append(tuple(where))
    return result.at[spots[0]].set(least).at[spots[1]].set(high)


def levels(own_key, dims, pieces, low, largest):
    def one(axis_at, blocks):
        draws = jax.random.uniform(jax.random.fold_in(jax.random.fold_in(own_key, 6), axis_at), (blocks,), jnp.float32, low / len(pieces), largest / len(pieces))
        return jnp.repeat(jnp.exp(draws), dims[axis_at] // blocks).reshape((-1,) + (1,) * (len(dims) - axis_at - 1))

    gain = one(*pieces[0])
    for cut in pieces[1:]:
        gain = gain * one(*cut)
    return gain


def profile(count, total, bound, skew):
    loads = [(1 << 20) // math.isqrt(rank ** skew) + 1 for rank in range(2, count + 1)]
    surplus, counts = total - bound - (count - 1), [1] * (count - 1)
    while surplus > 0:
        free = [i for i in range(count - 1) if counts[i] < bound]
        mass, left = sum([loads[i] for i in free]), surplus
        for i in free:
            extra = min(bound - counts[i], max(1, left * loads[i] // mass), surplus)
            counts[i] = counts[i] + extra
            surplus = surplus - extra
    return np.array([bound] + counts)


def uneven(rng, amount, total, limit, slope):
    if amount == 2:
        one = jax.random.randint(rng, (), max(1, total - limit), min(limit, total - 1) + 1)
        return jnp.stack([one, total - one])
    lengths = jnp.asarray(profile(amount, total, limit, slope), jnp.int32)
    couples = (amount - 1) // 2
    donor, taker = lengths[1:1 + 2 * couples:2], lengths[2:2 + 2 * couples:2]
    room = jnp.minimum(donor - 1, limit - taker)
    moved = jax.random.randint(jax.random.fold_in(rng, 1), (couples,), 0, 1 << 20) % (room + 1)
    lengths = lengths.at[1:1 + 2 * couples:2].set(donor - moved).at[2:2 + 2 * couples:2].set(taker + moved)
    return lengths[jax.random.permutation(jax.random.fold_in(rng, 2), amount)]


def bell_draw(stream_key, shape, spread, reach, cuts=(), kind=jnp.bfloat16):
    entries = jax.random.normal(stream_key, shape, jnp.float32) * spread
    if len(cuts) > 0:
        entries = levels(stream_key, shape, cuts, -0.22, 0.18) * entries
    return jnp.clip(entries, min=-reach, max=reach).astype(kind)


def setup_inputs(seed: int = 0) -> dict:
    streams_of = jax.random.split(jax.random.key(seed), 12)
    return {
        "response_rows": bell_draw(streams_of[0], (RESP_TOK, D), 1.0, 6.0, ((0, 32),)),
        "prompt_rows": bell_draw(streams_of[1], (PROMPT_ROWS, D), 1.0, 6.0, ((0, 32),)),
        "queries": draw_queries(jax.random.fold_in(streams_of[11], 71), 0),
        "response_keys": bell_draw(streams_of[3], (RESP_TOK, KV_HEADS * HEAD_DIM), 1.0, 6.0, ((0, 32),)),
        "prompt_keys": draw_prompt_keys(jax.random.fold_in(streams_of[11], 71), 0),
        "cotangent": bell_draw(streams_of[5], (RESP_TOK, HEADS * HEAD_DIM), 16.0, 96.0, ((0, 32),)),
        "segment_index": jax.vmap(lambda own: jnp.searchsorted(jnp.cumsum(uneven(own, RESPONSES, RESP_DEV, RESP_MOST, 0)), jnp.arange(RESP_DEV), side="right"))(jax.random.split(streams_of[6], (N_GROUP * N_SAMPLE))).reshape((N_GROUP * N_SAMPLE, RESP_DEV)).astype(jnp.int32),
        "prompt_choice": touch_ends(jax.random.randint(streams_of[7], (N_GROUP * N_SAMPLE, RESPONSES), 0, PROMPTS), jax.random.fold_in(streams_of[7], 1), 0, PROMPTS - 1).astype(jnp.int32),
        "frozen_value_weight": bell_draw(streams_of[8], (D, KV_HEADS * HEAD_DIM), D ** -0.5, 0.09375, ((0, 8),)),
        "value_adapter_down": bell_draw(streams_of[9], (D, RANK), D ** -0.5, 0.09375, ((0, 8),)),
        "value_adapter_up": bell_draw(streams_of[10], (RANK, KV_HEADS * HEAD_DIM), RANK ** -0.5, 1.5),
    }


adapter_scale = 2.0


def project(row_block, frozen_value_weight, value_adapter_down, value_adapter_up):
    down_projection = jnp.dot(row_block, value_adapter_down, preferred_element_type=jnp.float32).astype(jnp.bfloat16)
    value_inputs = jnp.dot(row_block, frozen_value_weight, preferred_element_type=jnp.float32)
    value_inputs = value_inputs + adapter_scale * jnp.dot(down_projection, value_adapter_up, preferred_element_type=jnp.float32)
    return down_projection, value_inputs.astype(jnp.bfloat16)


def visibility(segments, choices, prompt_total):
    tokens_here = segments.shape[0]
    onehot = (segments[:, None] == jnp.arange(choices.shape[0], dtype=jnp.int32)[None, :]).astype(jnp.int32)
    token_prompt = jnp.sum(onehot * choices[None, :], axis=1)
    key_prompt = jnp.arange(prompt_total, dtype=jnp.int32) // PROMPT_LEN
    prompt_seen = token_prompt[:, None] == key_prompt[None, :]
    position = jnp.arange(tokens_here, dtype=jnp.int32)
    own_seen = (segments[:, None] == segments[None, :]) & (position[None, :] <= position[:, None])
    return jnp.concatenate([prompt_seen, own_seen], axis=1)


def attend(query_rows, cotangent_rows, key_rows, value_rows, visible):
    tokens_here = query_rows.shape[0]
    key_total = key_rows.shape[0]
    group_size = HEADS // KV_HEADS
    score_scale = HEAD_DIM ** -0.5
    query_heads = query_rows.reshape(tokens_here, KV_HEADS, group_size, HEAD_DIM).astype(jnp.float32)
    cotangent_heads = cotangent_rows.reshape(tokens_here, KV_HEADS, group_size, HEAD_DIM).astype(jnp.float32)
    key_heads = key_rows.reshape(key_total, KV_HEADS, HEAD_DIM).astype(jnp.float32)
    value_heads = value_rows.reshape(key_total, KV_HEADS, HEAD_DIM).astype(jnp.float32)
    scores = jnp.einsum('tkgd,skd->kgts', query_heads, key_heads) * score_scale
    scores = jnp.where(visible[None, None], scores, -1e30)
    row_top = jnp.max(scores, axis=-1, keepdims=True)
    powers = jnp.exp(scores - row_top)
    softmax_full = powers / jnp.sum(powers, axis=-1, keepdims=True)
    softmax_low = lax.optimization_barrier(softmax_full.astype(jnp.bfloat16)).astype(jnp.float32)
    mixture = jnp.einsum('kgts,skd->kgtd', softmax_low, value_heads)
    row_delta = jnp.einsum('tkgd,kgtd->kgt', cotangent_heads, mixture)
    grad_softmax = jnp.einsum('tkgd,skd->kgts', cotangent_heads, value_heads)
    grad_scores = softmax_full * (grad_softmax - row_delta[..., None])
    grad_low = lax.optimization_barrier(grad_scores.astype(jnp.bfloat16)).astype(jnp.float32)
    key_grads = jnp.einsum('kgts,tkgd->skd', grad_low, query_heads) * score_scale
    value_grads = jnp.einsum('kgts,tkgd->skd', softmax_low, cotangent_heads)
    return (key_grads.reshape(key_total, KV_HEADS * HEAD_DIM),
            value_grads.reshape(key_total, KV_HEADS * HEAD_DIM))


def contract_final_axis(left, right):
    return lax.dot_general(left, right, (((1,), (1,)), ((), ())), preferred_element_type=jnp.float32)


def contract_first(left, right):
    return lax.dot_general(left, right, (((0,), (0,)), ((), ())), preferred_element_type=jnp.float32)


def back_project(value_low_rank, row_block, down_projection, frozen_value_weight, value_adapter_down, value_adapter_up):
    low_rank_backward = contract_final_axis(value_low_rank, value_adapter_up).astype(jnp.bfloat16)
    output_gradient = contract_final_axis(value_low_rank, frozen_value_weight) + adapter_scale * contract_final_axis(low_rank_backward, value_adapter_down)
    first_part = contract_first(row_block, low_rank_backward)
    second_part = contract_first(down_projection, value_low_rank)
    return output_gradient.astype(jnp.bfloat16), first_part, second_part


def reference(response_rows, prompt_rows, queries, response_keys, prompt_keys, cotangent, segment_index, prompt_choice, frozen_value_weight, value_adapter_down, value_adapter_up):
    kv_width = KV_HEADS * HEAD_DIM
    group_prompt = PROMPTS * PROMPT_LEN
    response_split = response_rows.reshape(N_GROUP, N_SAMPLE, RESP_DEV, D)
    query_split = queries.reshape(N_GROUP, N_SAMPLE, RESP_DEV, HEADS * HEAD_DIM)
    rkey_split = response_keys.reshape(N_GROUP, N_SAMPLE, RESP_DEV, kv_width)
    cot_split = cotangent.reshape(N_GROUP, N_SAMPLE, RESP_DEV, HEADS * HEAD_DIM)
    seg_split = segment_index.reshape(N_GROUP, N_SAMPLE, RESP_DEV)
    choice_split = prompt_choice.reshape(N_GROUP, N_SAMPLE, RESPONSES)
    prompt_split = prompt_rows.reshape(N_GROUP, group_prompt, D)
    pkey_split = prompt_keys.reshape(N_GROUP, group_prompt, kv_width)

    def one_group(items):
        g_resp, g_query, g_rkey, g_cot, g_seg, g_choice, g_prompt, g_pkey = items
        p_first, p_values = project(g_prompt, frozen_value_weight, value_adapter_down, value_adapter_up)

        def one_device(inner):
            row_block, query_block, rkey_block, cot_block, seg_block, choice_block = inner
            r_first, r_values = project(row_block, frozen_value_weight, value_adapter_down, value_adapter_up)
            visible = visibility(seg_block, choice_block, group_prompt)
            key_rows = jnp.concatenate([g_pkey, rkey_block], axis=0)
            value_rows = jnp.concatenate([p_values, r_values], axis=0)
            key_grads, value_grads = attend(query_block, cot_block, key_rows, value_rows, visible)
            value_low_rank = value_grads[group_prompt:].astype(jnp.bfloat16)
            output_gradient, first_part, second_part = back_project(value_low_rank, row_block, r_first, frozen_value_weight, value_adapter_down, value_adapter_up)
            return (output_gradient, key_grads[group_prompt:].astype(jnp.bfloat16), key_grads[:group_prompt],
                    value_grads[:group_prompt], first_part, second_part)

        output_gradient, rkey_grads, pkey_parts, pvalue_parts, first_parts, second_parts = lax.map(
            one_device, (g_resp, g_query, g_rkey, g_cot, g_seg, g_choice))
        prompt_value_low = jnp.sum(pvalue_parts, axis=0).astype(jnp.bfloat16)
        prompt_key_low = jnp.sum(pkey_parts, axis=0).astype(jnp.bfloat16)
        p_grads, p_first_part, p_second_part = back_project(prompt_value_low, g_prompt, p_first, frozen_value_weight, value_adapter_down, value_adapter_up)
        return (output_gradient, p_grads, rkey_grads, prompt_key_low,
                jnp.sum(first_parts, axis=0) + p_first_part, jnp.sum(second_parts, axis=0) + p_second_part)

    output_gradient, p_grads, rkey_grads, pkey_grads, first_sums, second_sums = lax.map(
        one_group, (response_split, query_split, rkey_split, cot_split, seg_split, choice_split, prompt_split, pkey_split))
    adapter_factor = adapter_scale * TOKEN_TOTAL ** -0.5
    return (output_gradient.reshape(RESP_TOK, D), p_grads.reshape(PROMPT_ROWS, D),
            rkey_grads.reshape(RESP_TOK, kv_width), pkey_grads.reshape(PROMPT_ROWS, kv_width),
            jnp.sum(first_sums, axis=0) * adapter_factor, jnp.sum(second_sums, axis=0) * adapter_factor)
```

```python
import functools

import jax
import jax.numpy as jnp
from jax import lax
from jax.experimental import pallas as pl
from jax.experimental.pallas import tpu as pltpu
from jax.sharding import PartitionSpec as P

HEADS = 32
KV_HEADS = 4
HEAD_DIM = 128
PROMPT_LEN = 128
GROUP_SIZE = HEADS // KV_HEADS
SCORE_SCALE = HEAD_DIM ** (-0.5)

adapter_scale = 2.0

BF = jnp.bfloat16
F32 = jnp.float32
MESH = pl.DeviceIdType.MESH


def nt(left, right):
    return lax.dot_general(left, right, (((1,), (1,)), ((), ())), preferred_element_type=F32)


def tn(left, right):
    return lax.dot_general(left, right, (((0,), (0,)), ((), ())), preferred_element_type=F32)


def nn(left, right):
    return lax.dot_general(left, right, (((1,), (0,)), ((), ())), preferred_element_type=F32)


class Slots:
    def __init__(self):
        self.count = 0

    def take(self, number):
        base = self.count
        self.count += number
        return base


def layout(nz, n_group):
    slots = Slots()
    places = {name: slots.take(nz) for name in (
        "k_z", "k_c", "d_z", "d_c", "v_z", "v_c",
        "w_z", "w_c", "w_x", "w_y", "w_d0", "w_d1",
        "rv_z", "rk_z", "ra_z",
    )}
    for name in ("rv_c", "rk_c", "ra_c"):
        places[name] = slots.take(1)
    places["g"] = slots.take(n_group)
    places["local"] = slots.take(4)
    return places, slots.count


def kernel(
    nz, n_group, places, factor,
    xr, xp, q, ct, w, rk, pk, seg, ch, dn, up,
    o_rg, o_pg, o_rk, o_pk, o_f, o_s,
    xv, qv, cv, wfull, kall, vall, dall, pmask, obias, prob, vlow, vloc, vp, acc, low,
    gv, gv_p, gv_h, gv_r, gk, gk_p, gk_h, gk_r, ga, ga_p, ga_h, ga_r, gg,
    ssem, rsem,
):
    g = lax.axis_index("group")
    j = lax.axis_index("sample")
    z = j // 2
    c = j % 2
    oc = 1 - c
    tokens = q.shape[0]
    rows = pk.shape[0]
    shard = w.shape[0]
    quarter = shard // 4
    half = quarter // 2
    prompts = 2 * nz * rows // PROMPT_LEN
    nzp = PROMPT_LEN // rows // 2
    partner = (g, j + 1 - 2 * c)
    gx = g + 1 - 2 * (g % 2)
    gy = g + 2 - 4 * ((g // 2) % 2)
    qme, qx, qy = g % 4, gx % 4, gy % 4
    qd = 3 - qme

    def zat(dz):
        return lax.rem(z + dz, nz)

    def zdev(dz):
        return (g, 2 * zat(dz) + c)

    def rcopy(src, dst, name, send, recv, device):
        return pltpu.make_async_remote_copy(
            src_ref=src, dst_ref=dst,
            send_sem=ssem.at[places[name] + send], recv_sem=rsem.at[places[name] + recv],
            device_id=device, device_id_type=MESH,
        )

    sends = []

    def go(copy):
        copy.start()
        sends.append(copy)

    def gather_start(src, buf, name_z, name_c):
        for dz in range(1, nz):
            go(rcopy(src, buf.at[z, c], name_z, dz, nz - dz, zdev(dz)))
        go(rcopy(src, buf.at[z, c], name_c, 0, 0, partner))

    def gather_forward(buf, name_z, name_c):
        for dz in range(1, nz):
            there = buf.at[zat(dz), c]
            rcopy(there, there, name_z, dz, dz, zdev(dz)).wait_recv()
            go(rcopy(there, there, name_c, dz, dz, partner))

    def gather_finish(buf, name_c):
        for dz in range(nz):
            there = buf.at[zat(dz), oc]
            rcopy(there, there, name_c, dz, dz, partner).wait_recv()

    def scatter_pair(part, pair, name_c):
        go(rcopy(part.at[:, oc], pair, name_c, 0, 0, partner))

    def scatter_z(part, pair, held, slots, name_c, name_z):
        rcopy(part.at[:, oc], pair, name_c, 0, 0, partner).wait_recv()
        held[...] = (part[:, c].astype(F32) + pair[...].astype(F32)).astype(BF)
        for dz in range(1, nz):
            go(rcopy(held.at[zat(dz)], slots.at[z], name_z, dz, nz - dz, zdev(dz)))
        slots[z] = held[z]

    def scatter_sum(slots, name_z):
        for dz in range(1, nz):
            there = slots.at[zat(dz)]
            rcopy(there, there, name_z, dz, dz, zdev(dz)).wait_recv()
        total = slots[0].astype(F32)
        for at in range(1, nz):
            total = total + slots[at].astype(F32)
        return total

    local = [
        pltpu.make_async_copy(src, dst, ssem.at[places["local"] + at])
        for at, (src, dst) in enumerate((
            (q, qv), (ct, cv), (xr, xv.at[pl.ds(0, tokens)]), (xp, xv.at[pl.ds(tokens, rows)])))
    ]
    for copy in local:
        copy.start()

    barrier = pltpu.get_barrier_semaphore()
    for dz in range(1, nz):
        pl.semaphore_signal(barrier, inc=1, device_id=zdev(dz), device_id_type=MESH)
    pl.semaphore_signal(barrier, inc=1, device_id=partner, device_id_type=MESH)
    for dg in range(1, n_group):
        pl.semaphore_signal(barrier, inc=1, device_id=(lax.rem(g + dg, n_group), j), device_id_type=MESH)
    pl.semaphore_wait(barrier, nz + n_group - 1)

    gather_start(pk, kall, "k_z", "k_c")
    mine = pl.ds(pl.multiple_of(qme * quarter, 16), quarter)
    for dz in range(1, nz):
        go(rcopy(w.at[mine], wfull.at[z, c, mine], "w_z", dz, nz - dz, zdev(dz)))
    go(rcopy(w, wfull.at[z, c], "w_c", 0, 0, partner))
    own_w = pltpu.make_async_copy(w, wfull.at[z, c], ssem.at[places["w_z"]])
    own_w.start()

    dall[z, c] = dn[...]
    gather_start(dn, dall, "d_z", "d_c")
    kall[z, c] = pk[...]

    seg_row = jnp.broadcast_to(seg[...], (tokens, tokens)).astype(F32)
    seg_col = jnp.transpose(seg_row)
    token = lax.broadcasted_iota(jnp.int32, (tokens, tokens), 0)
    other = lax.broadcasted_iota(jnp.int32, (tokens, tokens), 1)
    obias[...] = jnp.where((seg_row == seg_col) & (other <= token), 0.0, -1e30)
    choice = jnp.zeros((tokens, tokens), jnp.int32)
    for at in range(ch.shape[1]):
        choice = jnp.where(seg_col == float(at), ch[0, at], choice)
    for at in range(prompts):
        pmask[at] = jnp.where(choice == at, 1.0, 0.0).astype(BF)

    gather_forward(kall, "k_z", "k_c")
    local[0].wait()
    local[1].wait()
    gather_finish(kall, "k_c")

    def stack(ref, head):
        return [ref[:, pl.ds(pl.multiple_of((head * GROUP_SIZE + at) * HEAD_DIM, HEAD_DIM), HEAD_DIM)]
                for at in range(GROUP_SIZE)]

    def masked(parts):
        return jnp.concatenate(
            [jnp.concatenate([part * pmask[at] for part in parts], axis=0) for at in range(prompts)], axis=1)

    def side(buf, lanes):
        return jnp.concatenate(
            [buf[at * nzp:(at + 1) * nzp, :, :, lanes].reshape(PROMPT_LEN, HEAD_DIM) for at in range(prompts)],
            axis=1)

    def head_lanes(head):
        return pl.ds(pl.multiple_of(head * HEAD_DIM, HEAD_DIM), HEAD_DIM)

    def spread(buf, lanes, block):
        for at in range(prompts):
            buf[at * nzp:(at + 1) * nzp, :, :, lanes] = block[
                :, at * HEAD_DIM:(at + 1) * HEAD_DIM].astype(BF).reshape(nzp, 2, rows, HEAD_DIM)

    def softmax_head(head, carry):
        lanes = head_lanes(head)
        qs = stack(qv, head)
        s_sel = nt(masked(qs), side(kall, lanes)) * SCORE_SCALE
        s_own = nt(jnp.concatenate(qs, axis=0), rk[:, lanes]) * SCORE_SCALE
        s_own = s_own + jnp.concatenate([obias[...]] * GROUP_SIZE, axis=0)
        top = jnp.max(jnp.maximum(s_sel, s_own), axis=-1, keepdims=True)
        e_sel = jnp.exp(s_sel - top)
        e_own = jnp.exp(s_own - top)
        inv = 1.0 / jnp.sum(e_sel + e_own, axis=-1, keepdims=True)
        p_sel = e_sel * inv
        p_own = e_own * inv
        prob[head, :, 0:PROMPT_LEN] = p_sel
        prob[head, :, PROMPT_LEN:] = p_own
        cs = stack(cv, head)
        spread(gv, lanes, tn(p_sel.astype(BF), masked(cs)))
        vlow[0:tokens, lanes] = tn(p_own.astype(BF), jnp.concatenate(cs, axis=0)).astype(BF)
        return carry

    def w_plane(dz):
        there = wfull.at[zat(dz), c, mine]
        rcopy(there, there, "w_z", dz, dz, zdev(dz)).wait_recv()
        go(rcopy(there, there, "w_x", dz, dz, (gx, j)))
        go(rcopy(there, there, "w_y", dz, dz, (gy, j)))

    def w_diagonal(dz):
        at_x = pl.ds(pl.multiple_of(qx * quarter, 16), quarter)
        at_y = pl.ds(pl.multiple_of(qy * quarter, 16), quarter)
        there = wfull.at[zat(dz), c, at_x]
        rcopy(there, there, "w_x", dz, dz, (gx, j)).wait_recv()
        first = wfull.at[zat(dz), c, pl.ds(pl.multiple_of(qx * quarter, 16), half)]
        go(rcopy(first, first, "w_d0", dz, dz, (gy, j)))
        there = wfull.at[zat(dz), c, at_y]
        rcopy(there, there, "w_y", dz, dz, (gy, j)).wait_recv()
        second = wfull.at[zat(dz), c, pl.ds(pl.multiple_of(qy * quarter + half, 16), half)]
        go(rcopy(second, second, "w_d1", dz, dz, (gx, j)))

    def w_chip(dz):
        first = wfull.at[zat(dz), c, pl.ds(pl.multiple_of(qd * quarter, 16), half)]
        rcopy(first, first, "w_d0", dz, dz, (gy, j)).wait_recv()
        second = wfull.at[zat(dz), c, pl.ds(pl.multiple_of(qd * quarter + half, 16), half)]
        rcopy(second, second, "w_d1", dz, dz, (gx, j)).wait_recv()
        there = wfull.at[zat(dz), c]
        go(rcopy(there, there, "w_c", dz, dz, partner))

    lax.fori_loop(0, KV_HEADS // 2, softmax_head, 0)
    for dz in range(1, nz):
        w_plane(dz)
    lax.fori_loop(KV_HEADS // 2, KV_HEADS, softmax_head, 0)
    scatter_pair(gv, gv_p, "rv_c")
    for dz in range(1, nz):
        w_diagonal(dz)
    gather_forward(dall, "d_z", "d_c")
    scatter_z(gv, gv_p, gv_h, gv_r, "rv_c", "rv_z")
    local[2].wait()
    local[3].wait()
    own_w.wait()
    gather_finish(dall, "d_c")

    def columns(z_at, c_at):
        return pl.ds(pl.multiple_of((2 * z_at + c_at) * shard, 128), shard)

    def forward(z_at, c_at, first):
        x = xv[:, columns(z_at, c_at)]
        base = nn(x, wfull[z_at, c_at])
        lowest = nt(x, dall[z_at, c_at])
        acc[...] = base if first else acc[...] + base
        low[...] = lowest if first else low[...] + lowest

    forward(z, c, True)
    for dz in range(1, nz):
        w_chip(dz)
        forward(zat(dz), c, False)
    for dz in range(nz):
        there = wfull.at[zat(dz), oc]
        rcopy(there, there, "w_c", dz, dz, partner).wait_recv()
        forward(zat(dz), oc, False)
    first_proj = low[...].astype(BF)
    values = (acc[...] + adapter_scale * nn(first_proj, up[...])).astype(BF)
    vp[...] = values[tokens:]
    vloc[...] = values[:tokens]
    vall[z, c] = values[tokens:]
    gather_start(vp, vall, "v_z", "v_c")

    def back(first_row, count, out):
        rows_here = vlow[first_row:first_row + count]
        back_low = nt(rows_here, up[...]).astype(BF)

        def one(at, carry):
            z_at, c_at = at // 2, at % 2
            out[:, columns(z_at, c_at)] = (
                nt(rows_here, wfull[z_at, c_at]) + adapter_scale * nn(back_low, dall[z_at, c_at])).astype(BF)
            return carry

        lax.fori_loop(0, 2 * nz, one, 0)

    back(0, tokens, o_rg)
    vlow[tokens:] = scatter_sum(gv_r, "rv_z").astype(BF)
    back_all = nt(vlow[...], up[...]).astype(BF)
    second = tn(first_proj, vlow[...]).astype(BF)

    def adapter(at, carry):
        z_at, c_at = at // 2, at % 2
        ga[z_at, c_at, :, 0:shard] = tn(back_all, xv[:, columns(z_at, c_at)]).astype(BF)
        ga[z_at, c_at, :, shard:] = second
        return carry

    lax.fori_loop(0, 2 * nz, adapter, 0)
    scatter_pair(ga, ga_p, "ra_c")
    back(tokens, rows, o_pg)
    gather_forward(vall, "v_z", "v_c")
    scatter_z(ga, ga_p, ga_h, ga_r, "ra_c", "ra_z")
    gather_finish(vall, "v_c")

    def key_head(head, carry):
        lanes = head_lanes(head)
        cs = stack(cv, head)
        d_sel = nt(masked(cs), side(vall, lanes))
        d_own = nt(jnp.concatenate(cs, axis=0), vloc[:, lanes])
        p_sel = prob[head, :, 0:PROMPT_LEN]
        p_own = prob[head, :, PROMPT_LEN:]
        delta = jnp.sum(p_sel.astype(BF).astype(F32) * d_sel + p_own.astype(BF).astype(F32) * d_own,
                        axis=-1, keepdims=True)
        g_sel = (p_sel * (d_sel - delta)).astype(BF)
        g_own = (p_own * (d_own - delta)).astype(BF)
        qs = stack(qv, head)
        spread(gk, lanes, tn(g_sel, masked(qs)) * SCORE_SCALE)
        o_rk[:, lanes] = (tn(g_own, jnp.concatenate(qs, axis=0)) * SCORE_SCALE).astype(BF)
        return carry

    lax.fori_loop(0, KV_HEADS, key_head, 0)
    scatter_pair(gk, gk_p, "rk_c")
    gg[g] = scatter_sum(ga_r, "ra_z").astype(BF)
    for dg in range(1, n_group):
        there = lax.rem(g + dg, n_group)
        go(rcopy(gg.at[g], gg.at[g], "g", dg, n_group - dg, (there, j)))
    scatter_z(gk, gk_p, gk_h, gk_r, "rk_c", "rk_z")
    for dg in range(1, n_group):
        there = lax.rem(g + dg, n_group)
        rcopy(gg.at[there], gg.at[there], "g", dg, dg, (there, j)).wait_recv()
    total = gg[0].astype(F32)
    for at in range(1, n_group):
        total = total + gg[at].astype(F32)
    total = total * factor
    o_f[...] = total[:, 0:shard]
    o_s[...] = total[:, shard:]
    o_pk[...] = scatter_sum(gk_r, "rk_z").astype(BF)
    for copy in sends:
        copy.wait_send()


def on_device(
    n_group, n_sample,
    response_rows, prompt_rows, queries, response_keys, prompt_keys, cotangent,
    segment_index, prompt_choice, frozen_value_weight, value_adapter_down, value_adapter_up,
):
    tokens, d = response_rows.shape
    rows, kv = prompt_keys.shape
    shard, rank = value_adapter_down.shape
    nz = n_sample // 2
    places, count = layout(nz, n_group)
    factor = adapter_scale * float((tokens + rows) * n_group * n_sample) ** (-0.5)
    wide = shard + kv
    any_space = pl.BlockSpec(memory_space=pl.ANY)
    vmem = pl.BlockSpec(memory_space=pltpu.VMEM)
    smem = pl.BlockSpec(memory_space=pltpu.SMEM)

    def reduce_space(high, across):
        return [
            pltpu.VMEM((nz, 2, high, across), BF),
            pltpu.VMEM((nz, high, across), BF),
            pltpu.VMEM((nz, high, across), BF),
            pltpu.VMEM((nz, high, across), BF),
        ]

    outs = pl.pallas_call(
        functools.partial(kernel, nz, n_group, places, factor),
        out_shape=(
            jax.ShapeDtypeStruct((tokens, d), BF),
            jax.ShapeDtypeStruct((rows, d), BF),
            jax.ShapeDtypeStruct((tokens, kv), BF),
            jax.ShapeDtypeStruct((rows, kv), BF),
            jax.ShapeDtypeStruct((rank, shard), F32),
            jax.ShapeDtypeStruct((rank, kv), F32),
        ),
        in_specs=[any_space] * 5 + [vmem] * 3 + [smem] + [vmem] * 2,
        out_specs=(vmem,) * 6,
        scratch_shapes=[
            pltpu.VMEM((tokens + rows, d), BF),
            pltpu.VMEM((tokens, HEADS * HEAD_DIM), BF),
            pltpu.VMEM((tokens, HEADS * HEAD_DIM), BF),
            pltpu.VMEM((nz, 2, shard, kv), BF),
            pltpu.VMEM((nz, 2, rows, kv), BF),
            pltpu.VMEM((nz, 2, rows, kv), BF),
            pltpu.VMEM((nz, 2, rank, shard), BF),
            pltpu.VMEM((n_sample * rows // PROMPT_LEN, tokens, HEAD_DIM), BF),
            pltpu.VMEM((tokens, tokens), F32),
            pltpu.VMEM((KV_HEADS, GROUP_SIZE * tokens, PROMPT_LEN + tokens), F32),
            pltpu.VMEM((tokens + rows, kv), BF),
            pltpu.VMEM((tokens, kv), BF),
            pltpu.VMEM((rows, kv), BF),
            pltpu.VMEM((tokens + rows, kv), F32),
            pltpu.VMEM((tokens + rows, rank), F32),
            *reduce_space(rows, kv),
            *reduce_space(rows, kv),
            *reduce_space(rank, wide),
            pltpu.VMEM((n_group, rank, wide), BF),
            pltpu.SemaphoreType.DMA((count,)),
            pltpu.SemaphoreType.DMA((count,)),
        ],
        compiler_params=pltpu.CompilerParams(
            collective_id=0, has_side_effects=True, vmem_limit_bytes=56 * 1024 * 1024
        ),
        name="value_backward",
    )(
        response_rows, prompt_rows, queries, cotangent, frozen_value_weight,
        response_keys, prompt_keys, segment_index, prompt_choice, value_adapter_down.T, value_adapter_up,
    )
    return (*outs[:4], outs[4].T, outs[5])


def solution(mesh):
    both = P(("group", "sample"), None)
    in_specs = (both,) * 8 + (P("sample", None), P("sample", None), P())
    out_specs = (both,) * 4 + (P("sample", None), P())
    return jax.shard_map(
        functools.partial(on_device, mesh.shape["group"], mesh.shape["sample"]),
        mesh=mesh, in_specs=in_specs, out_specs=out_specs, check_vma=False,
    )
```

```python
import functools

import jax
import jax.numpy as jnp
from jax import lax
from jax.experimental import pallas as pl
from jax.experimental.pallas import tpu as pltpu
from jax.sharding import PartitionSpec as P

HEADS = 32
KV_HEADS = 4
HEAD_DIM = 128
PROMPT_LEN = 128
GROUP_SIZE = HEADS // KV_HEADS
SCORE_SCALE = HEAD_DIM ** (-0.5)

adapter_scale = 2.0

BF = jnp.bfloat16
F32 = jnp.float32
MESH = pl.DeviceIdType.MESH


def nt(left, right):
    return lax.dot_general(left, right, (((1,), (1,)), ((), ())), preferred_element_type=F32)


def tn(left, right):
    return lax.dot_general(left, right, (((0,), (0,)), ((), ())), preferred_element_type=F32)


def nn(left, right):
    return lax.dot_general(left, right, (((1,), (0,)), ((), ())), preferred_element_type=F32)


class Slots:
    def __init__(self):
        self.count = 0

    def take(self, number):
        base = self.count
        self.count += number
        return base


def layout(nz, n_group):
    slots = Slots()
    places = {name: slots.take(nz) for name in (
        "k_z", "k_c", "d_z", "d_c", "v_z", "v_c",
        "w_z", "w_c", "w_x", "w_y", "w_d0", "w_d1",
        "rv_z", "rk_z", "rk_z2", "ra_z",
    )}
    for name in ("rv_c", "rk_c", "rk_c2", "ra_c"):
        places[name] = slots.take(1)
    places["g"] = slots.take(n_group)
    places["local"] = slots.take(4)
    return places, slots.count


def kernel(
    nz, n_group, places, factor,
    xr, xp, q, ct, w, rk, pk, seg, ch, dn, up,
    o_rg, o_pg, o_rk, o_pk, o_f, o_s,
    xv, qv, cv, wfull, kall, vall, dall, pmask, obias, prob, vlow, vloc, vp, acc, low,
    gv, gv_p, gv_h, gv_r, gk, gk_p, gk_h, gk_r, ga, ga_p, ga_h, ga_r, gg,
    ssem, rsem,
):
    g = lax.axis_index("group")
    j = lax.axis_index("sample")
    z = j // 2
    c = j % 2
    oc = 1 - c
    tokens = q.shape[0]
    rows = pk.shape[0]
    shard = w.shape[0]
    quarter = shard // 4
    half = quarter // 2
    prompts = 2 * nz * rows // PROMPT_LEN
    nzp = PROMPT_LEN // rows // 2
    partner = (g, j + 1 - 2 * c)
    gx = g + 1 - 2 * (g % 2)
    gy = g + 2 - 4 * ((g // 2) % 2)
    qme, qx, qy = g % 4, gx % 4, gy % 4
    qd = 3 - qme

    def zat(dz):
        return lax.rem(z + dz, nz)

    def zdev(dz):
        return (g, 2 * zat(dz) + c)

    def rcopy(src, dst, name, send, recv, device):
        return pltpu.make_async_remote_copy(
            src_ref=src, dst_ref=dst,
            send_sem=ssem.at[places[name] + send], recv_sem=rsem.at[places[name] + recv],
            device_id=device, device_id_type=MESH,
        )

    near = [dz for dz in range(1, nz) if dz in (1, nz - 1)]
    far = [dz for dz in range(1, nz) if dz not in near]
    sends = []

    def go(copy):
        copy.start()
        sends.append(copy)

    def gather_start(src, buf, name_z, name_c):
        for dz in range(1, nz):
            go(rcopy(src, buf.at[z, c], name_z, dz, nz - dz, zdev(dz)))
        go(rcopy(src, buf.at[z, c], name_c, 0, 0, partner))

    def gather_forward(buf, name_z, name_c):
        for dz in range(1, nz):
            there = buf.at[zat(dz), c]
            rcopy(there, there, name_z, dz, dz, zdev(dz)).wait_recv()
            go(rcopy(there, there, name_c, dz, dz, partner))

    def gather_finish(buf, name_c):
        for dz in range(nz):
            there = buf.at[zat(dz), oc]
            rcopy(there, there, name_c, dz, dz, partner).wait_recv()

    def scatter_pair(part, pair, name_c):
        go(rcopy(part.at[:, oc], pair, name_c, 0, 0, partner))

    def scatter_z(part, pair, held, slots, name_c, name_z):
        rcopy(part.at[:, oc], pair, name_c, 0, 0, partner).wait_recv()
        held[...] = (part[:, c].astype(F32) + pair[...].astype(F32)).astype(BF)
        for dz in range(1, nz):
            go(rcopy(held.at[zat(dz)], slots.at[z], name_z, dz, nz - dz, zdev(dz)))
        slots[z] = held[z]

    def scatter_sum(slots, name_z):
        for dz in range(1, nz):
            there = slots.at[zat(dz)]
            rcopy(there, there, name_z, dz, dz, zdev(dz)).wait_recv()
        total = slots[0].astype(F32)
        for at in range(1, nz):
            total = total + slots[at].astype(F32)
        return total

    local = [
        pltpu.make_async_copy(src, dst, ssem.at[places["local"] + at])
        for at, (src, dst) in enumerate((
            (q, qv), (ct, cv), (xr, xv.at[pl.ds(0, tokens)]), (xp, xv.at[pl.ds(tokens, rows)])))
    ]
    for copy in local:
        copy.start()

    barrier = pltpu.get_barrier_semaphore()
    for dz in range(1, nz):
        pl.semaphore_signal(barrier, inc=1, device_id=zdev(dz), device_id_type=MESH)
    pl.semaphore_signal(barrier, inc=1, device_id=partner, device_id_type=MESH)
    for dg in range(1, n_group):
        pl.semaphore_signal(barrier, inc=1, device_id=(lax.rem(g + dg, n_group), j), device_id_type=MESH)
    pl.semaphore_wait(barrier, nz + n_group - 1)

    gather_start(pk, kall, "k_z", "k_c")
    mine = pl.ds(pl.multiple_of(qme * quarter, 16), quarter)
    for dz in near + far:
        go(rcopy(w.at[mine], wfull.at[z, c, mine], "w_z", dz, nz - dz, zdev(dz)))
    go(rcopy(w, wfull.at[z, c], "w_c", 0, 0, partner))
    own_w = pltpu.make_async_copy(w, wfull.at[z, c], ssem.at[places["w_z"]])
    own_w.start()

    dall[z, c] = dn[...]
    gather_start(dn, dall, "d_z", "d_c")
    kall[z, c] = pk[...]

    seg_row = jnp.broadcast_to(seg[...], (tokens, tokens)).astype(F32)
    seg_col = jnp.transpose(seg_row)
    token = lax.broadcasted_iota(jnp.int32, (tokens, tokens), 0)
    other = lax.broadcasted_iota(jnp.int32, (tokens, tokens), 1)
    obias[...] = jnp.where((seg_row == seg_col) & (token <= other), 0.0, -1e30)
    choice = jnp.zeros((tokens, tokens), jnp.int32)
    for at in range(ch.shape[1]):
        choice = jnp.where(seg_col == float(at), ch[0, at], choice)
    for at in range(prompts):
        pmask[at] = jnp.where(choice == at, 1.0, 0.0).astype(BF)

    gather_forward(kall, "k_z", "k_c")
    local[0].wait()
    local[1].wait()
    gather_finish(kall, "k_c")

    def stack(ref, head):
        return [ref[:, pl.ds(pl.multiple_of((head * GROUP_SIZE + at) * HEAD_DIM, HEAD_DIM), HEAD_DIM)]
                for at in range(GROUP_SIZE)]

    def masked(parts):
        return jnp.concatenate(
            [jnp.concatenate([part * pmask[at] for part in parts], axis=0) for at in range(prompts)], axis=1)

    def side(buf, lanes):
        return jnp.concatenate(
            [buf[at * nzp:(at + 1) * nzp, :, :, lanes].reshape(PROMPT_LEN, HEAD_DIM) for at in range(prompts)],
            axis=1)

    def head_lanes(head):
        return pl.ds(pl.multiple_of(head * HEAD_DIM, HEAD_DIM), HEAD_DIM)

    def spread(buf, lanes, block):
        for at in range(prompts):
            buf[at * nzp:(at + 1) * nzp, :, :, lanes] = block[
                :, at * HEAD_DIM:(at + 1) * HEAD_DIM].astype(BF).reshape(nzp, 2, rows, HEAD_DIM)

    def softmax_head(head):
        lanes = head_lanes(head)
        qs = stack(qv, head)
        s_sel = nt(side(kall, lanes), masked(qs)) * SCORE_SCALE
        s_own = nt(rk[:, lanes], jnp.concatenate(qs, axis=0)) * SCORE_SCALE
        s_own = s_own + jnp.concatenate([obias[...]] * GROUP_SIZE, axis=1)
        top = jnp.max(jnp.maximum(s_sel, s_own), axis=0, keepdims=True)
        e_sel = jnp.exp(s_sel - top)
        e_own = jnp.exp(s_own - top)
        inv = 1.0 / jnp.sum(e_sel + e_own, axis=0, keepdims=True)
        p_sel = e_sel * inv
        p_own = e_own * inv
        prob[head, 0:PROMPT_LEN] = p_sel
        prob[head, PROMPT_LEN:] = p_own
        cs = stack(cv, head)
        spread(gv, lanes, nn(p_sel.astype(BF), masked(cs)))
        vlow[0:tokens, lanes] = nn(p_own.astype(BF), jnp.concatenate(cs, axis=0)).astype(BF)

    def w_plane(dz):
        there = wfull.at[zat(dz), c, mine]
        rcopy(there, there, "w_z", dz, dz, zdev(dz)).wait_recv()
        go(rcopy(there, there, "w_x", dz, dz, (gx, j)))
        go(rcopy(there, there, "w_y", dz, dz, (gy, j)))

    def w_diagonal(dz):
        at_x = pl.ds(pl.multiple_of(qx * quarter, 16), quarter)
        at_y = pl.ds(pl.multiple_of(qy * quarter, 16), quarter)
        there = wfull.at[zat(dz), c, at_x]
        rcopy(there, there, "w_x", dz, dz, (gx, j)).wait_recv()
        first = wfull.at[zat(dz), c, pl.ds(pl.multiple_of(qx * quarter, 16), half)]
        go(rcopy(first, first, "w_d0", dz, dz, (gy, j)))
        there = wfull.at[zat(dz), c, at_y]
        rcopy(there, there, "w_y", dz, dz, (gy, j)).wait_recv()
        second = wfull.at[zat(dz), c, pl.ds(pl.multiple_of(qy * quarter + half, 16), half)]
        go(rcopy(second, second, "w_d1", dz, dz, (gx, j)))

    def w_chip(dz):
        first = wfull.at[zat(dz), c, pl.ds(pl.multiple_of(qd * quarter, 16), half)]
        rcopy(first, first, "w_d0", dz, dz, (gy, j)).wait_recv()
        second = wfull.at[zat(dz), c, pl.ds(pl.multiple_of(qd * quarter + half, 16), half)]
        rcopy(second, second, "w_d1", dz, dz, (gx, j)).wait_recv()
        there = wfull.at[zat(dz), c]
        go(rcopy(there, there, "w_c", dz, dz, partner))

    softmax_head(0)
    for dz in near:
        w_plane(dz)
    softmax_head(1)
    for dz in far:
        w_plane(dz)
    softmax_head(2)
    for dz in near:
        w_diagonal(dz)
    softmax_head(3)
    scatter_pair(gv, gv_p, "rv_c")
    for dz in far:
        w_diagonal(dz)
    gather_forward(dall, "d_z", "d_c")
    scatter_z(gv, gv_p, gv_h, gv_r, "rv_c", "rv_z")
    local[2].wait()
    local[3].wait()
    own_w.wait()
    gather_finish(dall, "d_c")

    def columns(z_at, c_at):
        return pl.ds(pl.multiple_of((2 * z_at + c_at) * shard, 128), shard)

    def forward(z_at, c_at, first):
        x = xv[:, columns(z_at, c_at)]
        base = nn(x, wfull[z_at, c_at])
        lowest = nt(x, dall[z_at, c_at])
        acc[...] = base if first else acc[...] + base
        low[...] = lowest if first else low[...] + lowest

    forward(z, c, True)
    for dz in near + far:
        w_chip(dz)
        forward(zat(dz), c, False)
    for dz in [0] + near + far:
        there = wfull.at[zat(dz), oc]
        rcopy(there, there, "w_c", dz, dz, partner).wait_recv()
        forward(zat(dz), oc, False)
    first_proj = low[...].astype(BF)
    values = (acc[...] + adapter_scale * nn(first_proj, up[...])).astype(BF)
    vp[...] = values[tokens:]
    vloc[...] = values[:tokens]
    vall[z, c] = values[tokens:]
    gather_start(vp, vall, "v_z", "v_c")

    vlow[tokens:] = scatter_sum(gv_r, "rv_z").astype(BF)
    back_all = nt(vlow[...], up[...]).astype(BF)
    second = tn(first_proj, vlow[...]).astype(BF)

    def adapter(at, carry):
        z_at, c_at = at // 2, at % 2
        ga[z_at, c_at, :, 0:shard] = tn(back_all, xv[:, columns(z_at, c_at)]).astype(BF)
        ga[z_at, c_at, :, shard:] = second
        return carry

    lax.fori_loop(0, 2 * nz, adapter, 0)
    scatter_pair(ga, ga_p, "ra_c")

    def back(at, carry):
        z_at, c_at = at // 2, at % 2
        grad = (nt(vlow[...], wfull[z_at, c_at]) + adapter_scale * nn(back_all, dall[z_at, c_at])).astype(BF)
        o_rg[:, columns(z_at, c_at)] = grad[:tokens]
        o_pg[:, columns(z_at, c_at)] = grad[tokens:]
        return carry

    lax.fori_loop(0, 2 * nz, back, 0)
    gather_forward(vall, "v_z", "v_c")
    scatter_z(ga, ga_p, ga_h, ga_r, "ra_c", "ra_z")
    gather_finish(vall, "v_c")

    def key_head(head, carry):
        lanes = head_lanes(head)
        cs = stack(cv, head)
        d_sel = nt(side(vall, lanes), masked(cs))
        d_own = nt(vloc[:, lanes], jnp.concatenate(cs, axis=0))
        p_sel = prob[head, 0:PROMPT_LEN]
        p_own = prob[head, PROMPT_LEN:]
        delta = jnp.sum(p_sel.astype(BF).astype(F32) * d_sel + p_own.astype(BF).astype(F32) * d_own,
                        axis=0, keepdims=True)
        g_sel = (p_sel * (d_sel - delta)).astype(BF)
        g_own = (p_own * (d_own - delta)).astype(BF)
        qs = stack(qv, head)
        per_half = KV_HEADS // 2
        spread(gk.at[head // per_half], head_lanes(head % per_half), nn(g_sel, masked(qs)) * SCORE_SCALE)
        o_rk[:, lanes] = (nn(g_own, jnp.concatenate(qs, axis=0)) * SCORE_SCALE).astype(BF)
        return carry

    lax.fori_loop(0, KV_HEADS // 2, key_head, 0)
    scatter_pair(gk.at[0], gk_p.at[0], "rk_c")
    lax.fori_loop(KV_HEADS // 2, KV_HEADS, key_head, 0)
    scatter_pair(gk.at[1], gk_p.at[1], "rk_c2")
    scatter_z(gk.at[0], gk_p.at[0], gk_h.at[0], gk_r.at[0], "rk_c", "rk_z")
    gg[g] = scatter_sum(ga_r, "ra_z").astype(BF)
    for dg in range(1, n_group):
        there = lax.rem(g + dg, n_group)
        go(rcopy(gg.at[g], gg.at[g], "g", dg, n_group - dg, (there, j)))
    scatter_z(gk.at[1], gk_p.at[1], gk_h.at[1], gk_r.at[1], "rk_c2", "rk_z2")
    for dg in range(1, n_group):
        there = lax.rem(g + dg, n_group)
        rcopy(gg.at[there], gg.at[there], "g", dg, dg, (there, j)).wait_recv()
    total = gg[0].astype(F32)
    for at in range(1, n_group):
        total = total + gg[at].astype(F32)
    total = total * factor
    o_f[...] = total[:, 0:shard]
    o_s[...] = total[:, shard:]
    width = o_pk.shape[1] // 2
    o_pk[:, 0:width] = scatter_sum(gk_r.at[0], "rk_z").astype(BF)
    o_pk[:, width:] = scatter_sum(gk_r.at[1], "rk_z2").astype(BF)
    for copy in sends:
        copy.wait_send()


def store(*refs):
    sem = refs[12]
    copies = [pltpu.make_async_copy(refs[at], refs[6 + at], sem.at[at]) for at in range(6)]
    for copy in copies:
        copy.start()
    for copy in copies:
        copy.wait()


def on_device(
    n_group, n_sample,
    response_rows, prompt_rows, queries, response_keys, prompt_keys, cotangent,
    segment_index, prompt_choice, frozen_value_weight, value_adapter_down, value_adapter_up,
):
    tokens, d = response_rows.shape
    rows, kv = prompt_keys.shape
    shard, rank = value_adapter_down.shape
    nz = n_sample // 2
    places, count = layout(nz, n_group)
    factor = adapter_scale * float((tokens + rows) * n_group * n_sample) ** (-0.5)
    wide = shard + kv
    any_space = pl.BlockSpec(memory_space=pl.ANY)
    vmem = pl.BlockSpec(memory_space=pltpu.VMEM)
    smem = pl.BlockSpec(memory_space=pltpu.SMEM)

    def reduce_space(high, across, lead=()):
        return [
            pltpu.VMEM((*lead, nz, 2, high, across), BF),
            pltpu.VMEM((*lead, nz, high, across), BF),
            pltpu.VMEM((*lead, nz, high, across), BF),
            pltpu.VMEM((*lead, nz, high, across), BF),
        ]

    shapes = (
        ((tokens, d), BF), ((rows, d), BF), ((tokens, kv), BF), ((rows, kv), BF),
        ((rank, shard), F32), ((rank, kv), F32),
    )
    outs = pl.pallas_call(
        functools.partial(kernel, nz, n_group, places, factor),
        out_shape=tuple(pltpu.VMEM(shape, kind) for shape, kind in shapes),
        in_specs=[any_space] * 5 + [vmem] * 3 + [smem] + [vmem] * 2,
        out_specs=(vmem,) * 6,
        scratch_shapes=[
            pltpu.VMEM((tokens + rows, d), BF),
            pltpu.VMEM((tokens, HEADS * HEAD_DIM), BF),
            pltpu.VMEM((tokens, HEADS * HEAD_DIM), BF),
            pltpu.VMEM((nz, 2, shard, kv), BF),
            pltpu.VMEM((nz, 2, rows, kv), BF),
            pltpu.VMEM((nz, 2, rows, kv), BF),
            pltpu.VMEM((nz, 2, rank, shard), BF),
            pltpu.VMEM((n_sample * rows // PROMPT_LEN, tokens, HEAD_DIM), BF),
            pltpu.VMEM((tokens, tokens), F32),
            pltpu.VMEM((KV_HEADS, PROMPT_LEN + tokens, GROUP_SIZE * tokens), F32),
            pltpu.VMEM((tokens + rows, kv), BF),
            pltpu.VMEM((tokens, kv), BF),
            pltpu.VMEM((rows, kv), BF),
            pltpu.VMEM((tokens + rows, kv), F32),
            pltpu.VMEM((tokens + rows, rank), F32),
            *reduce_space(rows, kv),
            *reduce_space(rows, kv // 2, (2,)),
            *reduce_space(rank, wide),
            pltpu.VMEM((n_group, rank, wide), BF),
            pltpu.SemaphoreType.DMA((count,)),
            pltpu.SemaphoreType.DMA((count,)),
        ],
        compiler_params=pltpu.CompilerParams(
            collective_id=0, has_side_effects=True, vmem_limit_bytes=56 * 1024 * 1024
        ),
        name="value_backward",
    )(
        response_rows, prompt_rows, queries, cotangent, frozen_value_weight,
        response_keys, prompt_keys, segment_index, prompt_choice, value_adapter_down.T, value_adapter_up,
    )
    outs = pl.pallas_call(
        store,
        out_shape=tuple(jax.ShapeDtypeStruct(shape, kind) for shape, kind in shapes),
        in_specs=[any_space] * 6,
        out_specs=(any_space,) * 6,
        scratch_shapes=[pltpu.SemaphoreType.DMA((6,))],
        name="store",
    )(*outs)
    return (*outs[:4], outs[4].T, outs[5])


def solution(mesh):
    both = P(("group", "sample"), None)
    in_specs = (both,) * 8 + (P("sample", None), P("sample", None), P())
    out_specs = (both,) * 4 + (P("sample", None), P())
    return jax.shard_map(
        functools.partial(on_device, mesh.shape["group"], mesh.shape["sample"]),
        mesh=mesh, in_specs=in_specs, out_specs=out_specs, check_vma=False,
    )
```

```python
import functools

import jax
import jax.numpy as jnp
from jax import lax
from jax.experimental import pallas as pl
from jax.experimental.pallas import tpu as pltpu
from jax.sharding import PartitionSpec as P

HEADS = 32
KV_HEADS = 4
HEAD_DIM = 128
PROMPT_LEN = 128
GROUP_SIZE = HEADS // KV_HEADS
SCORE_SCALE = HEAD_DIM ** (-0.5)

adapter_scale = 2.0

BF = jnp.bfloat16
F32 = jnp.float32
MESH = pl.DeviceIdType.MESH


def nt(left, right):
    return lax.dot_general(left, right, (((1,), (1,)), ((), ())), preferred_element_type=F32)


def tn(left, right):
    return lax.dot_general(left, right, (((0,), (0,)), ((), ())), preferred_element_type=F32)


def nn(left, right):
    return lax.dot_general(left, right, (((1,), (0,)), ((), ())), preferred_element_type=F32)


class Slots:
    def __init__(self):
        self.count = 0

    def take(self, number):
        base = self.count
        self.count += number
        return base


def layout(nz, n_group):
    slots = Slots()
    places = {name: slots.take(nz) for name in (
        "k_z", "k_c", "d_z", "d_c", "v_z", "v_c",
        "w_z", "w_c", "w_x", "w_y", "w_d0", "w_d1",
        "rv_z", "rk_z", "rk_z2", "ra_z",
    )}
    for name in ("rv_c", "rk_c", "rk_c2", "ra_c"):
        places[name] = slots.take(1)
    places["g"] = slots.take(n_group)
    places["local"] = slots.take(4)
    return places, slots.count


def kernel(
    nz, n_group, places, factor,
    xr, xp, q, ct, w, rk, pk, seg, ch, dn, up,
    o_rg, o_pg, o_rk, o_pk, o_f, o_s,
    xv, qv, cv, wfull, kall, vall, dall, pmask, obias, prob, vlow, vloc, vp, acc, low,
    gv, gv_p, gv_h, gv_r, gk, gk_p, gk_h, gk_r, ga, ga_p, ga_h, ga_r, gg,
    ssem, rsem,
):
    g = lax.axis_index("group")
    j = lax.axis_index("sample")
    z = j // 2
    c = j % 2
    oc = 1 - c
    tokens = q.shape[0]
    rows = pk.shape[0]
    shard = w.shape[0]
    quarter = shard // 4
    half = quarter // 2
    prompts = 2 * nz * rows // PROMPT_LEN
    nzp = PROMPT_LEN // rows // 2
    partner = (g, j + 1 - 2 * c)
    gx = g + 1 - 2 * (g % 2)
    gy = g + 2 - 4 * ((g // 2) % 2)
    qme, qx, qy = g % 4, gx % 4, gy % 4
    qd = 3 - qme

    def zat(dz):
        return lax.rem(z + dz, nz)

    def zdev(dz):
        return (g, 2 * zat(dz) + c)

    def rcopy(src, dst, name, send, recv, device):
        return pltpu.make_async_remote_copy(
            src_ref=src, dst_ref=dst,
            send_sem=ssem.at[places[name] + send], recv_sem=rsem.at[places[name] + recv],
            device_id=device, device_id_type=MESH,
        )

    near = [dz for dz in range(1, nz) if dz in (1, nz - 1)]
    far = [dz for dz in range(1, nz) if dz not in near]
    sends = []

    def go(copy):
        copy.start()
        sends.append(copy)

    def gather_start(src, buf, name_z, name_c):
        for dz in range(1, nz):
            go(rcopy(src, buf.at[z, c], name_z, dz, nz - dz, zdev(dz)))
        go(rcopy(src, buf.at[z, c], name_c, 0, 0, partner))

    def gather_forward(buf, name_z, name_c):
        for dz in range(1, nz):
            there = buf.at[zat(dz), c]
            rcopy(there, there, name_z, dz, dz, zdev(dz)).wait_recv()
            go(rcopy(there, there, name_c, dz, dz, partner))

    def gather_finish(buf, name_c):
        for dz in range(nz):
            there = buf.at[zat(dz), oc]
            rcopy(there, there, name_c, dz, dz, partner).wait_recv()

    def scatter_pair(part, pair, name_c):
        go(rcopy(part.at[:, oc], pair, name_c, 0, 0, partner))

    def scatter_z(part, pair, held, slots, name_c, name_z):
        rcopy(part.at[:, oc], pair, name_c, 0, 0, partner).wait_recv()
        held[...] = (part[:, c].astype(F32) + pair[...].astype(F32)).astype(BF)
        for dz in range(1, nz):
            go(rcopy(held.at[zat(dz)], slots.at[z], name_z, dz, nz - dz, zdev(dz)))
        slots[z] = held[z]

    def scatter_sum(slots, name_z):
        for dz in range(1, nz):
            there = slots.at[zat(dz)]
            rcopy(there, there, name_z, dz, dz, zdev(dz)).wait_recv()
        total = slots[0].astype(F32)
        for at in range(1, nz):
            total = total + slots[at].astype(F32)
        return total

    local = [
        pltpu.make_async_copy(src, dst, ssem.at[places["local"] + at])
        for at, (src, dst) in enumerate((
            (q, qv), (ct, cv), (xr, xv.at[pl.ds(0, tokens)]), (xp, xv.at[pl.ds(tokens, rows)])))
    ]
    for copy in local:
        copy.start()

    barrier = pltpu.get_barrier_semaphore()
    for dz in range(1, nz):
        pl.semaphore_signal(barrier, inc=1, device_id=zdev(dz), device_id_type=MESH)
    pl.semaphore_signal(barrier, inc=1, device_id=partner, device_id_type=MESH)
    for dg in range(1, n_group):
        pl.semaphore_signal(barrier, inc=1, device_id=(lax.rem(g + dg, n_group), j), device_id_type=MESH)
    pl.semaphore_wait(barrier, nz + n_group - 1)

    mine = pl.ds(pl.multiple_of(qme * quarter, 16), quarter)
    for dz in near + far:
        go(rcopy(w.at[mine], wfull.at[z, c, mine], "w_z", dz, nz - dz, zdev(dz)))
    go(rcopy(w, wfull.at[z, c], "w_c", 0, 0, partner))
    own_w = pltpu.make_async_copy(w, wfull.at[z, c], ssem.at[places["w_z"]])
    own_w.start()
    gather_start(pk, kall, "k_z", "k_c")

    dall[z, c] = dn[...]
    gather_start(dn, dall, "d_z", "d_c")
    kall[z, c] = pk[...]

    seg_row = jnp.broadcast_to(seg[...], (tokens, tokens)).astype(F32)
    seg_col = jnp.transpose(seg_row)
    token = lax.broadcasted_iota(jnp.int32, (tokens, tokens), 0)
    other = lax.broadcasted_iota(jnp.int32, (tokens, tokens), 1)
    obias[...] = jnp.where((seg_row == seg_col) & (token <= other), 0.0, -1e30)
    choice = jnp.zeros((tokens, tokens), jnp.int32)
    for at in range(ch.shape[1]):
        choice = jnp.where(seg_col == float(at), ch[0, at], choice)
    for at in range(prompts):
        pmask[at] = jnp.where(choice == at, 1.0, 0.0).astype(BF)

    def stack(ref, head):
        return [ref[:, pl.ds(pl.multiple_of((head * GROUP_SIZE + at) * HEAD_DIM, HEAD_DIM), HEAD_DIM)]
                for at in range(GROUP_SIZE)]

    def masked(parts):
        return jnp.concatenate(
            [jnp.concatenate([part * pmask[at] for part in parts], axis=0) for at in range(prompts)], axis=1)

    def side(buf, lanes):
        return jnp.concatenate(
            [buf[at * nzp:(at + 1) * nzp, :, :, lanes].reshape(PROMPT_LEN, HEAD_DIM) for at in range(prompts)],
            axis=1)

    def head_lanes(head):
        return pl.ds(pl.multiple_of(head * HEAD_DIM, HEAD_DIM), HEAD_DIM)

    def spread(buf, lanes, block):
        for at in range(prompts):
            buf[at * nzp:(at + 1) * nzp, :, :, lanes] = block[
                :, at * HEAD_DIM:(at + 1) * HEAD_DIM].astype(BF).reshape(nzp, 2, rows, HEAD_DIM)

    def softmax_head(head):
        lanes = head_lanes(head)
        qs = stack(qv, head)
        s_sel = nt(side(kall, lanes), masked(qs)) * SCORE_SCALE
        s_own = nt(rk[:, lanes], jnp.concatenate(qs, axis=0)) * SCORE_SCALE
        s_own = s_own + jnp.concatenate([obias[...]] * GROUP_SIZE, axis=1)
        top = jnp.max(jnp.maximum(s_sel, s_own), axis=0, keepdims=True)
        e_sel = jnp.exp(s_sel - top)
        e_own = jnp.exp(s_own - top)
        inv = 1.0 / jnp.sum(e_sel + e_own, axis=0, keepdims=True)
        p_sel = e_sel * inv
        p_own = e_own * inv
        prob[head, 0:PROMPT_LEN] = p_sel
        prob[head, PROMPT_LEN:] = p_own
        cs = stack(cv, head)
        spread(gv, lanes, nn(p_sel.astype(BF), masked(cs)))
        vlow[0:tokens, lanes] = nn(p_own.astype(BF), jnp.concatenate(cs, axis=0)).astype(BF)

    def w_plane(dz):
        there = wfull.at[zat(dz), c, mine]
        rcopy(there, there, "w_z", dz, dz, zdev(dz)).wait_recv()
        go(rcopy(there, there, "w_x", dz, dz, (gx, j)))
        go(rcopy(there, there, "w_y", dz, dz, (gy, j)))

    def w_diagonal(dz):
        at_x = pl.ds(pl.multiple_of(qx * quarter, 16), quarter)
        at_y = pl.ds(pl.multiple_of(qy * quarter, 16), quarter)
        there = wfull.at[zat(dz), c, at_x]
        rcopy(there, there, "w_x", dz, dz, (gx, j)).wait_recv()
        first = wfull.at[zat(dz), c, pl.ds(pl.multiple_of(qx * quarter, 16), half)]
        go(rcopy(first, first, "w_d0", dz, dz, (gy, j)))
        there = wfull.at[zat(dz), c, at_y]
        rcopy(there, there, "w_y", dz, dz, (gy, j)).wait_recv()
        second = wfull.at[zat(dz), c, pl.ds(pl.multiple_of(qy * quarter + half, 16), half)]
        go(rcopy(second, second, "w_d1", dz, dz, (gx, j)))

    def w_chip(dz):
        first = wfull.at[zat(dz), c, pl.ds(pl.multiple_of(qd * quarter, 16), half)]
        rcopy(first, first, "w_d0", dz, dz, (gy, j)).wait_recv()
        second = wfull.at[zat(dz), c, pl.ds(pl.multiple_of(qd * quarter + half, 16), half)]
        rcopy(second, second, "w_d1", dz, dz, (gx, j)).wait_recv()
        there = wfull.at[zat(dz), c]
        go(rcopy(there, there, "w_c", dz, dz, partner))

    def columns(z_at, c_at):
        return pl.ds(pl.multiple_of((2 * z_at + c_at) * shard, 128), shard)

    def forward(z_at, c_at, first):
        x = xv[:, columns(z_at, c_at)]
        base = nn(x, wfull[z_at, c_at])
        lowest = nt(x, dall[z_at, c_at])
        acc[...] = base if first else acc[...] + base
        low[...] = lowest if first else low[...] + lowest

    def forward_other(dz):
        there = wfull.at[zat(dz), oc]
        rcopy(there, there, "w_c", dz, dz, partner).wait_recv()
        forward(zat(dz), oc, False)

    for dz in near:
        w_plane(dz)
    gather_forward(dall, "d_z", "d_c")
    gather_finish(dall, "d_c")
    local[2].wait()
    local[3].wait()
    own_w.wait()
    forward(z, c, True)
    forward_other(0)
    for dz in far:
        w_plane(dz)
    for dz in near + far:
        w_diagonal(dz)
    gather_forward(kall, "k_z", "k_c")
    for dz in near + far:
        w_chip(dz)
        forward(zat(dz), c, False)
    for dz in near + far:
        forward_other(dz)
    first_proj = low[...].astype(BF)
    values = (acc[...] + adapter_scale * nn(first_proj, up[...])).astype(BF)
    vp[...] = values[tokens:]
    vloc[...] = values[:tokens]
    vall[z, c] = values[tokens:]
    gather_start(vp, vall, "v_z", "v_c")

    local[0].wait()
    local[1].wait()
    gather_finish(kall, "k_c")
    for head in range(KV_HEADS):
        softmax_head(head)
        if head == KV_HEADS // 2:
            gather_forward(vall, "v_z", "v_c")
    scatter_pair(gv, gv_p, "rv_c")
    gather_finish(vall, "v_c")
    scatter_z(gv, gv_p, gv_h, gv_r, "rv_c", "rv_z")

    def key_head(head, carry):
        lanes = head_lanes(head)
        cs = stack(cv, head)
        d_sel = nt(side(vall, lanes), masked(cs))
        d_own = nt(vloc[:, lanes], jnp.concatenate(cs, axis=0))
        p_sel = prob[head, 0:PROMPT_LEN]
        p_own = prob[head, PROMPT_LEN:]
        delta = jnp.sum(p_sel.astype(BF).astype(F32) * d_sel + p_own.astype(BF).astype(F32) * d_own,
                        axis=0, keepdims=True)
        g_sel = (p_sel * (d_sel - delta)).astype(BF)
        g_own = (p_own * (d_own - delta)).astype(BF)
        qs = stack(qv, head)
        per_half = KV_HEADS // 2
        spread(gk.at[head // per_half], head_lanes(head % per_half), nn(g_sel, masked(qs)) * SCORE_SCALE)
        o_rk[:, lanes] = (nn(g_own, jnp.concatenate(qs, axis=0)) * SCORE_SCALE).astype(BF)
        return carry

    lax.fori_loop(0, KV_HEADS // 2, key_head, 0)
    scatter_pair(gk.at[0], gk_p.at[0], "rk_c")

    vlow[tokens:] = scatter_sum(gv_r, "rv_z").astype(BF)
    back_all = nt(vlow[...], up[...]).astype(BF)
    second = tn(first_proj, vlow[...]).astype(BF)

    def adapter(at, carry):
        z_at, c_at = at // 2, at % 2
        ga[z_at, c_at, :, 0:shard] = tn(back_all, xv[:, columns(z_at, c_at)]).astype(BF)
        ga[z_at, c_at, :, shard:] = second
        return carry

    lax.fori_loop(0, 2 * nz, adapter, 0)
    scatter_pair(ga, ga_p, "ra_c")
    scatter_z(gk.at[0], gk_p.at[0], gk_h.at[0], gk_r.at[0], "rk_c", "rk_z")
    lax.fori_loop(KV_HEADS // 2, KV_HEADS, key_head, 0)
    scatter_pair(gk.at[1], gk_p.at[1], "rk_c2")
    scatter_z(ga, ga_p, ga_h, ga_r, "ra_c", "ra_z")
    scatter_z(gk.at[1], gk_p.at[1], gk_h.at[1], gk_r.at[1], "rk_c2", "rk_z2")

    def back(at, carry):
        z_at, c_at = at // 2, at % 2
        grad = (nt(vlow[...], wfull[z_at, c_at]) + adapter_scale * nn(back_all, dall[z_at, c_at])).astype(BF)
        o_rg[:, columns(z_at, c_at)] = grad[:tokens]
        o_pg[:, columns(z_at, c_at)] = grad[tokens:]
        return carry

    lax.fori_loop(0, nz, back, 0)
    gg[g] = scatter_sum(ga_r, "ra_z").astype(BF)
    for dg in range(1, n_group):
        there = lax.rem(g + dg, n_group)
        go(rcopy(gg.at[g], gg.at[g], "g", dg, n_group - dg, (there, j)))
    lax.fori_loop(nz, 2 * nz, back, 0)
    for dg in range(1, n_group):
        there = lax.rem(g + dg, n_group)
        rcopy(gg.at[there], gg.at[there], "g", dg, dg, (there, j)).wait_recv()
    total = gg[0].astype(F32)
    for at in range(1, n_group):
        total = total + gg[at].astype(F32)
    total = total * factor
    o_f[...] = total[:, 0:shard]
    o_s[...] = total[:, shard:]
    width = o_pk.shape[1] // 2
    o_pk[:, 0:width] = scatter_sum(gk_r.at[0], "rk_z").astype(BF)
    o_pk[:, width:] = scatter_sum(gk_r.at[1], "rk_z2").astype(BF)
    for copy in sends:
        copy.wait_send()


def store(*refs):
    sem = refs[12]
    copies = [pltpu.make_async_copy(refs[at], refs[6 + at], sem.at[at]) for at in range(6)]
    for copy in copies:
        copy.start()
    for copy in copies:
        copy.wait()


def on_device(
    n_group, n_sample,
    response_rows, prompt_rows, queries, response_keys, prompt_keys, cotangent,
    segment_index, prompt_choice, frozen_value_weight, value_adapter_down, value_adapter_up,
):
    tokens, d = response_rows.shape
    rows, kv = prompt_keys.shape
    shard, rank = value_adapter_down.shape
    nz = n_sample // 2
    places, count = layout(nz, n_group)
    factor = adapter_scale * float((tokens + rows) * n_group * n_sample) ** (-0.5)
    wide = shard + kv
    any_space = pl.BlockSpec(memory_space=pl.ANY)
    vmem = pl.BlockSpec(memory_space=pltpu.VMEM)
    smem = pl.BlockSpec(memory_space=pltpu.SMEM)

    def reduce_space(high, across, lead=()):
        return [
            pltpu.VMEM((*lead, nz, 2, high, across), BF),
            pltpu.VMEM((*lead, nz, high, across), BF),
            pltpu.VMEM((*lead, nz, high, across), BF),
            pltpu.VMEM((*lead, nz, high, across), BF),
        ]

    shapes = (
        ((tokens, d), BF), ((rows, d), BF), ((tokens, kv), BF), ((rows, kv), BF),
        ((rank, shard), F32), ((rank, kv), F32),
    )
    outs = pl.pallas_call(
        functools.partial(kernel, nz, n_group, places, factor),
        out_shape=tuple(pltpu.VMEM(shape, kind) for shape, kind in shapes),
        in_specs=[any_space] * 5 + [vmem] * 3 + [smem] + [vmem] * 2,
        out_specs=(vmem,) * 6,
        scratch_shapes=[
            pltpu.VMEM((tokens + rows, d), BF),
            pltpu.VMEM((tokens, HEADS * HEAD_DIM), BF),
            pltpu.VMEM((tokens, HEADS * HEAD_DIM), BF),
            pltpu.VMEM((nz, 2, shard, kv), BF),
            pltpu.VMEM((nz, 2, rows, kv), BF),
            pltpu.VMEM((nz, 2, rows, kv), BF),
            pltpu.VMEM((nz, 2, rank, shard), BF),
            pltpu.VMEM((n_sample * rows // PROMPT_LEN, tokens, HEAD_DIM), BF),
            pltpu.VMEM((tokens, tokens), F32),
            pltpu.VMEM((KV_HEADS, PROMPT_LEN + tokens, GROUP_SIZE * tokens), F32),
            pltpu.VMEM((tokens + rows, kv), BF),
            pltpu.VMEM((tokens, kv), BF),
            pltpu.VMEM((rows, kv), BF),
            pltpu.VMEM((tokens + rows, kv), F32),
            pltpu.VMEM((tokens + rows, rank), F32),
            *reduce_space(rows, kv),
            *reduce_space(rows, kv // 2, (2,)),
            *reduce_space(rank, wide),
            pltpu.VMEM((n_group, rank, wide), BF),
            pltpu.SemaphoreType.DMA((count,)),
            pltpu.SemaphoreType.DMA((count,)),
        ],
        compiler_params=pltpu.CompilerParams(
            collective_id=0, has_side_effects=True, vmem_limit_bytes=56 * 1024 * 1024
        ),
        name="value_backward",
    )(
        response_rows, prompt_rows, queries, cotangent, frozen_value_weight,
        response_keys, prompt_keys, segment_index, prompt_choice, value_adapter_down.T, value_adapter_up,
    )
    outs = pl.pallas_call(
        store,
        out_shape=tuple(jax.ShapeDtypeStruct(shape, kind) for shape, kind in shapes),
        in_specs=[vmem] * 6,
        out_specs=(pl.BlockSpec(memory_space=pltpu.HBM),) * 6,
        scratch_shapes=[pltpu.SemaphoreType.DMA((6,))],
        name="store",
    )(*outs)
    return (*outs[:4], outs[4].T, outs[5])


def solution(mesh):
    both = P(("group", "sample"), None)
    in_specs = (both,) * 8 + (P("sample", None), P("sample", None), P())
    out_specs = (both,) * 4 + (P("sample", None), P())
    return jax.shard_map(
        functools.partial(on_device, mesh.shape["group"], mesh.shape["sample"]),
        mesh=mesh, in_specs=in_specs, out_specs=out_specs, check_vma=False,
    )
```

```python
import functools

import jax
import jax.numpy as jnp
from jax import lax
from jax.experimental import pallas as pl
from jax.experimental.pallas import tpu as pltpu
from jax.sharding import PartitionSpec as P

HEADS = 32
KV_HEADS = 4
HEAD_DIM = 128
PROMPT_LEN = 128
GROUP_SIZE = HEADS // KV_HEADS
SCORE_SCALE = HEAD_DIM ** (-0.5)

adapter_scale = 2.0

BF = jnp.bfloat16
F32 = jnp.float32
MESH = pl.DeviceIdType.MESH


def nt(left, right):
    return lax.dot_general(left, right, (((1,), (1,)), ((), ())), preferred_element_type=F32)


def tn(left, right):
    return lax.dot_general(left, right, (((0,), (0,)), ((), ())), preferred_element_type=F32)


def nn(left, right):
    return lax.dot_general(left, right, (((1,), (0,)), ((), ())), preferred_element_type=F32)


class Slots:
    def __init__(self):
        self.count = 0

    def take(self, number):
        base = self.count
        self.count += number
        return base


def layout(nz, n_group):
    slots = Slots()
    places = {name: slots.take(nz) for name in (
        "k_z", "k_l", "k_c", "w_l", "d_z", "d_c", "v_z", "v_c",
        "w_z", "w_c", "w_x", "w_y", "w_d0", "w_d1",
        "rv_z", "rk_z", "rk_z2", "ra_z",
    )}
    for name in ("rv_c", "rk_c", "rk_c2", "ra_c"):
        places[name] = slots.take(1)
    places["g"] = slots.take(n_group)
    places["local"] = slots.take(5)
    return places, slots.count


def kernel(
    nz, n_group, places, factor,
    xr, xp, q, ct, w, rk, pk, seg, ch, dn, up,
    o_rg, o_pg, o_rk, o_pk, o_f, o_s,
    xv, qv, cv, wfull, kall, vall, dall, pmask, obias, prob, vlow, vloc, vp, acc, low,
    gv, gv_p, gv_h, gv_r, gk, gk_p, gk_h, gk_r, ga, ga_p, ga_h, ga_r, gg,
    ssem, rsem,
):
    g = lax.axis_index("group")
    j = lax.axis_index("sample")
    z = j // 2
    c = j % 2
    oc = 1 - c
    tokens = q.shape[0]
    rows = pk.shape[0]
    shard = w.shape[0]
    quarter = shard // 4
    half = quarter // 2
    prompts = 2 * nz * rows // PROMPT_LEN
    nzp = PROMPT_LEN // rows // 2
    partner = (g, j + 1 - 2 * c)
    gx = g + 1 - 2 * (g % 2)
    gy = g + 2 - 4 * ((g // 2) % 2)
    qme, qx, qy = g % 4, gx % 4, gy % 4
    qd = 3 - qme

    def zat(dz):
        return lax.rem(z + dz, nz)

    def zdev(dz):
        return (g, 2 * zat(dz) + c)

    def rcopy(src, dst, name, send, recv, device, recv_name=None):
        return pltpu.make_async_remote_copy(
            src_ref=src, dst_ref=dst,
            send_sem=ssem.at[places[name] + send], recv_sem=rsem.at[places[recv_name or name] + recv],
            device_id=device, device_id_type=MESH,
        )

    short = jnp.minimum(z, nz - 1 - z)

    def source(k):
        alternate = z + (k + 1) // 2 if k % 2 else z - k // 2
        one_side = jnp.where(2 * z < nz - 1, z + k - short, z - k + short)
        return jnp.where(k <= 2 * short, alternate, one_side)

    sources = [source(k) for k in range(1, nz)]

    sends = []

    def go(copy):
        copy.start()
        sends.append(copy)

    waits = []

    def go_if(condition, make):
        @pl.when(condition)
        def _():
            make().start()

        waits.append((condition, make))

    def chain_start(src, dst, name, name_left):
        go_if(z + 1 < nz, lambda: rcopy(src, dst, name, z, z, (g, jnp.minimum(j + 2, 2 * nz - 1))))
        go_if(z >= 1, lambda: rcopy(src, dst, name_left, z, z, (g, jnp.maximum(j - 2, 0)), name))

    def chain_next(there, name, src):
        rcopy(there, there, name, src, src, partner).wait_recv()
        after = jnp.where(src < z, z + 1, z - 1)
        inside = jnp.minimum(jnp.maximum(after, 0), nz - 1)
        go_if(after == inside, lambda: rcopy(there, there, name, src, src, (g, 2 * inside + c)))

    def gather_start(src, buf, name_z, name_c):
        for dz in range(1, nz):
            go(rcopy(src, buf.at[z, c], name_z, dz, nz - dz, zdev(dz)))
        go(rcopy(src, buf.at[z, c], name_c, 0, 0, partner))

    def gather_forward(buf, name_z, name_c):
        for dz in range(1, nz):
            there = buf.at[zat(dz), c]
            rcopy(there, there, name_z, dz, dz, zdev(dz)).wait_recv()
            go(rcopy(there, there, name_c, dz, dz, partner))

    def gather_finish(buf, name_c):
        for dz in range(nz):
            there = buf.at[zat(dz), oc]
            rcopy(there, there, name_c, dz, dz, partner).wait_recv()

    def scatter_pair(part, pair, name_c):
        go(rcopy(part.at[:, oc], pair, name_c, 0, 0, partner))

    def scatter_z(part, pair, held, slots, name_c, name_z):
        rcopy(part.at[:, oc], pair, name_c, 0, 0, partner).wait_recv()
        held[...] = (part[:, c].astype(F32) + pair[...].astype(F32)).astype(BF)
        for dz in range(1, nz):
            go(rcopy(held.at[zat(dz)], slots.at[z], name_z, dz, nz - dz, zdev(dz)))
        slots[z] = held[z]

    def scatter_sum(slots, name_z):
        for dz in range(1, nz):
            there = slots.at[zat(dz)]
            rcopy(there, there, name_z, dz, dz, zdev(dz)).wait_recv()
        total = slots[0].astype(F32)
        for at in range(1, nz):
            total = total + slots[at].astype(F32)
        return total

    local = [
        pltpu.make_async_copy(src, dst, ssem.at[places["local"] + at])
        for at, (src, dst) in enumerate((
            (q, qv), (ct, cv), (xr, xv.at[pl.ds(0, tokens)]), (xp, xv.at[pl.ds(tokens, rows)])))
    ]
    for copy in local:
        copy.start()

    barrier = pltpu.get_barrier_semaphore()
    for dz in range(1, nz):
        pl.semaphore_signal(barrier, inc=1, device_id=zdev(dz), device_id_type=MESH)
    pl.semaphore_signal(barrier, inc=1, device_id=partner, device_id_type=MESH)
    for dg in range(1, n_group):
        pl.semaphore_signal(barrier, inc=1, device_id=(lax.rem(g + dg, n_group), j), device_id_type=MESH)
    pl.semaphore_wait(barrier, nz + n_group - 1)

    mine = pl.ds(pl.multiple_of(qme * quarter, 16), quarter)
    chain_start(pk, kall.at[z, c], "k_z", "k_l")
    go(rcopy(pk, kall.at[z, c], "k_c", z, z, partner))
    chain_start(w.at[mine], wfull.at[z, c, mine], "w_z", "w_l")
    go(rcopy(w, wfull.at[z, c], "w_c", z, z, partner))
    own_w = pltpu.make_async_copy(w, wfull.at[z, c], ssem.at[places["local"] + 4])
    own_w.start()

    dall[z, c] = dn[...]
    gather_start(dn, dall, "d_z", "d_c")
    kall[z, c] = pk[...]

    seg_row = jnp.broadcast_to(seg[...], (tokens, tokens)).astype(F32)
    seg_col = jnp.transpose(seg_row)
    token = lax.broadcasted_iota(jnp.int32, (tokens, tokens), 0)
    other = lax.broadcasted_iota(jnp.int32, (tokens, tokens), 1)
    obias[...] = jnp.where((seg_row == seg_col) & (token <= other), 0.0, -1e30)
    choice = jnp.zeros((tokens, tokens), jnp.int32)
    for at in range(ch.shape[1]):
        choice = jnp.where(seg_col == float(at), ch[0, at], choice)
    for at in range(prompts):
        pmask[at] = jnp.where(choice == at, 1.0, 0.0).astype(BF)

    def stack(ref, head):
        return [ref[:, pl.ds(pl.multiple_of((head * GROUP_SIZE + at) * HEAD_DIM, HEAD_DIM), HEAD_DIM)]
                for at in range(GROUP_SIZE)]

    def masked(parts):
        return jnp.concatenate(
            [jnp.concatenate([part * pmask[at] for part in parts], axis=0) for at in range(prompts)], axis=1)

    def side(buf, lanes):
        return jnp.concatenate(
            [buf[at * nzp:(at + 1) * nzp, :, :, lanes].reshape(PROMPT_LEN, HEAD_DIM) for at in range(prompts)],
            axis=1)

    def head_lanes(head):
        return pl.ds(pl.multiple_of(head * HEAD_DIM, HEAD_DIM), HEAD_DIM)

    def spread(buf, lanes, block):
        for at in range(prompts):
            buf[at * nzp:(at + 1) * nzp, :, :, lanes] = block[
                :, at * HEAD_DIM:(at + 1) * HEAD_DIM].astype(BF).reshape(nzp, 2, rows, HEAD_DIM)

    def softmax_head(head):
        lanes = head_lanes(head)
        qs = stack(qv, head)
        s_sel = nt(side(kall, lanes), masked(qs)) * SCORE_SCALE
        s_own = nt(rk[:, lanes], jnp.concatenate(qs, axis=0)) * SCORE_SCALE
        s_own = s_own + jnp.concatenate([obias[...]] * GROUP_SIZE, axis=1)
        top = jnp.max(jnp.maximum(s_sel, s_own), axis=0, keepdims=True)
        e_sel = jnp.exp(s_sel - top)
        e_own = jnp.exp(s_own - top)
        inv = 1.0 / jnp.sum(e_sel + e_own, axis=0, keepdims=True)
        p_sel = e_sel * inv
        p_own = e_own * inv
        prob[head, 0:PROMPT_LEN] = p_sel
        prob[head, PROMPT_LEN:] = p_own
        cs = stack(cv, head)
        spread(gv, lanes, nn(p_sel.astype(BF), masked(cs)))
        vlow[0:tokens, lanes] = nn(p_own.astype(BF), jnp.concatenate(cs, axis=0)).astype(BF)

    def w_plane(src):
        there = wfull.at[src, c, mine]
        chain_next(there, "w_z", src)
        go(rcopy(there, there, "w_x", src, src, (gx, j)))
        go(rcopy(there, there, "w_y", src, src, (gy, j)))

    def w_diagonal(src):
        there = wfull.at[src, c, pl.ds(pl.multiple_of(qx * quarter, 16), quarter)]
        rcopy(there, there, "w_x", src, src, (gx, j)).wait_recv()
        first = wfull.at[src, c, pl.ds(pl.multiple_of(qx * quarter, 16), half)]
        go(rcopy(first, first, "w_d0", src, src, (gy, j)))
        there = wfull.at[src, c, pl.ds(pl.multiple_of(qy * quarter, 16), quarter)]
        rcopy(there, there, "w_y", src, src, (gy, j)).wait_recv()
        second = wfull.at[src, c, pl.ds(pl.multiple_of(qy * quarter + half, 16), half)]
        go(rcopy(second, second, "w_d1", src, src, (gx, j)))

    def w_chip(src):
        first = wfull.at[src, c, pl.ds(pl.multiple_of(qd * quarter, 16), half)]
        rcopy(first, first, "w_d0", src, src, (gy, j)).wait_recv()
        second = wfull.at[src, c, pl.ds(pl.multiple_of(qd * quarter + half, 16), half)]
        rcopy(second, second, "w_d1", src, src, (gx, j)).wait_recv()
        there = wfull.at[src, c]
        go(rcopy(there, there, "w_c", src, src, partner))

    for src in sources:
        there = kall.at[src, c]
        chain_next(there, "k_z", src)
        go(rcopy(there, there, "k_c", src, src, partner))
    local[0].wait()
    local[1].wait()
    for at in range(nz):
        there = kall.at[at, oc]
        rcopy(there, there, "k_c", at, at, partner).wait_recv()

    stages = []
    for at in range(nz + 1):
        if at < nz - 1:
            stages.append(functools.partial(w_plane, sources[at]))
        if 0 <= at - 1 < nz - 1:
            stages.append(functools.partial(w_diagonal, sources[at - 1]))
        if 0 <= at - 2 < nz - 1:
            stages.append(functools.partial(w_chip, sources[at - 2]))
    per_head = -(-len(stages) // (KV_HEADS + 1))
    for head in range(KV_HEADS):
        for stage in stages[head * per_head:(head + 1) * per_head]:
            stage()
        softmax_head(head)
    scatter_pair(gv, gv_p, "rv_c")
    for stage in stages[KV_HEADS * per_head:]:
        stage()
    gather_forward(dall, "d_z", "d_c")
    scatter_z(gv, gv_p, gv_h, gv_r, "rv_c", "rv_z")
    gather_finish(dall, "d_c")
    local[2].wait()
    local[3].wait()
    own_w.wait()

    def columns(z_at, c_at):
        return pl.ds(pl.multiple_of((2 * z_at + c_at) * shard, 128), shard)

    def forward(z_at, c_at, first):
        x = xv[:, columns(z_at, c_at)]
        base = nn(x, wfull[z_at, c_at])
        lowest = nt(x, dall[z_at, c_at])
        acc[...] = base if first else acc[...] + base
        low[...] = lowest if first else low[...] + lowest

    forward(z, c, True)
    for src in sources:
        forward(src, c, False)
    for src in [z] + sources:
        there = wfull.at[src, oc]
        rcopy(there, there, "w_c", src, src, partner).wait_recv()
        forward(src, oc, False)
    first_proj = low[...].astype(BF)
    values = (acc[...] + adapter_scale * nn(first_proj, up[...])).astype(BF)
    vp[...] = values[tokens:]
    vloc[...] = values[:tokens]
    vall[z, c] = values[tokens:]
    gather_start(vp, vall, "v_z", "v_c")

    vlow[tokens:] = scatter_sum(gv_r, "rv_z").astype(BF)
    back_all = nt(vlow[...], up[...]).astype(BF)
    second = tn(first_proj, vlow[...]).astype(BF)

    def adapter(at, carry):
        z_at, c_at = at // 2, at % 2
        ga[z_at, c_at, :, 0:shard] = tn(back_all, xv[:, columns(z_at, c_at)]).astype(BF)
        ga[z_at, c_at, :, shard:] = second
        return carry

    lax.fori_loop(0, 2 * nz, adapter, 0)
    scatter_pair(ga, ga_p, "ra_c")

    def back(at, carry):
        z_at, c_at = at // 2, at % 2
        grad = (nt(vlow[...], wfull[z_at, c_at]) + adapter_scale * nn(back_all, dall[z_at, c_at])).astype(BF)
        o_rg[:, columns(z_at, c_at)] = grad[:tokens]
        o_pg[:, columns(z_at, c_at)] = grad[tokens:]
        return carry

    lax.fori_loop(0, nz, back, 0)
    gather_forward(vall, "v_z", "v_c")
    scatter_z(ga, ga_p, ga_h, ga_r, "ra_c", "ra_z")
    gather_finish(vall, "v_c")

    def key_head(head, carry):
        lanes = head_lanes(head)
        cs = stack(cv, head)
        d_sel = nt(side(vall, lanes), masked(cs))
        d_own = nt(vloc[:, lanes], jnp.concatenate(cs, axis=0))
        p_sel = prob[head, 0:PROMPT_LEN]
        p_own = prob[head, PROMPT_LEN:]
        delta = jnp.sum(p_sel.astype(BF).astype(F32) * d_sel + p_own.astype(BF).astype(F32) * d_own,
                        axis=0, keepdims=True)
        g_sel = (p_sel * (d_sel - delta)).astype(BF)
        g_own = (p_own * (d_own - delta)).astype(BF)
        qs = stack(qv, head)
        per_half = KV_HEADS // 2
        spread(gk.at[head // per_half], head_lanes(head % per_half), nn(g_sel, masked(qs)) * SCORE_SCALE)
        o_rk[:, lanes] = (nn(g_own, jnp.concatenate(qs, axis=0)) * SCORE_SCALE).astype(BF)
        return carry

    lax.fori_loop(0, KV_HEADS // 2, key_head, 0)
    scatter_pair(gk.at[0], gk_p.at[0], "rk_c")
    lax.fori_loop(KV_HEADS // 2, KV_HEADS - 1, key_head, 0)
    scatter_z(gk.at[0], gk_p.at[0], gk_h.at[0], gk_r.at[0], "rk_c", "rk_z")
    gg[g] = scatter_sum(ga_r, "ra_z").astype(BF)
    for dg in range(1, n_group):
        there = lax.rem(g + dg, n_group)
        go(rcopy(gg.at[g], gg.at[g], "g", dg, n_group - dg, (there, j)))
    lax.fori_loop(KV_HEADS - 1, KV_HEADS, key_head, 0)
    scatter_pair(gk.at[1], gk_p.at[1], "rk_c2")
    scatter_z(gk.at[1], gk_p.at[1], gk_h.at[1], gk_r.at[1], "rk_c2", "rk_z2")
    lax.fori_loop(nz, 2 * nz, back, 0)
    for dg in range(1, n_group):
        there = lax.rem(g + dg, n_group)
        rcopy(gg.at[there], gg.at[there], "g", dg, dg, (there, j)).wait_recv()
    total = gg[0].astype(F32)
    for at in range(1, n_group):
        total = total + gg[at].astype(F32)
    total = total * factor
    o_f[...] = total[:, 0:shard]
    o_s[...] = total[:, shard:]
    width = o_pk.shape[1] // 2
    o_pk[:, 0:width] = scatter_sum(gk_r.at[0], "rk_z").astype(BF)
    o_pk[:, width:] = scatter_sum(gk_r.at[1], "rk_z2").astype(BF)
    for copy in sends:
        copy.wait_send()
    for condition, make in waits:
        @pl.when(condition)
        def _():
            make().wait_send()


def store(*refs):
    sem = refs[12]
    copies = [pltpu.make_async_copy(refs[at], refs[6 + at], sem.at[at]) for at in range(6)]
    for copy in copies:
        copy.start()
    for copy in copies:
        copy.wait()


def on_device(
    n_group, n_sample,
    response_rows, prompt_rows, queries, response_keys, prompt_keys, cotangent,
    segment_index, prompt_choice, frozen_value_weight, value_adapter_down, value_adapter_up,
):
    tokens, d = response_rows.shape
    rows, kv = prompt_keys.shape
    shard, rank = value_adapter_down.shape
    nz = n_sample // 2
    places, count = layout(nz, n_group)
    factor = adapter_scale * float((tokens + rows) * n_group * n_sample) ** (-0.5)
    wide = shard + kv
    any_space = pl.BlockSpec(memory_space=pl.ANY)
    vmem = pl.BlockSpec(memory_space=pltpu.VMEM)
    smem = pl.BlockSpec(memory_space=pltpu.SMEM)

    def reduce_space(high, across, lead=()):
        return [
            pltpu.VMEM((*lead, nz, 2, high, across), BF),
            pltpu.VMEM((*lead, nz, high, across), BF),
            pltpu.VMEM((*lead, nz, high, across), BF),
            pltpu.VMEM((*lead, nz, high, across), BF),
        ]

    shapes = (
        ((tokens, d), BF), ((rows, d), BF), ((tokens, kv), BF), ((rows, kv), BF),
        ((rank, shard), F32), ((rank, kv), F32),
    )
    outs = pl.pallas_call(
        functools.partial(kernel, nz, n_group, places, factor),
        out_shape=tuple(jax.ShapeDtypeStruct(shape, kind) for shape, kind in shapes),
        in_specs=[any_space] * 5 + [vmem] * 3 + [smem] + [vmem] * 2,
        out_specs=(vmem,) * 6,
        scratch_shapes=[
            pltpu.VMEM((tokens + rows, d), BF),
            pltpu.VMEM((tokens, HEADS * HEAD_DIM), BF),
            pltpu.VMEM((tokens, HEADS * HEAD_DIM), BF),
            pltpu.VMEM((nz, 2, shard, kv), BF),
            pltpu.VMEM((nz, 2, rows, kv), BF),
            pltpu.VMEM((nz, 2, rows, kv), BF),
            pltpu.VMEM((nz, 2, rank, shard), BF),
            pltpu.VMEM((n_sample * rows // PROMPT_LEN, tokens, HEAD_DIM), BF),
            pltpu.VMEM((tokens, tokens), F32),
            pltpu.VMEM((KV_HEADS, PROMPT_LEN + tokens, GROUP_SIZE * tokens), F32),
            pltpu.VMEM((tokens + rows, kv), BF),
            pltpu.VMEM((tokens, kv), BF),
            pltpu.VMEM((rows, kv), BF),
            pltpu.VMEM((tokens + rows, kv), F32),
            pltpu.VMEM((tokens + rows, rank), F32),
            *reduce_space(rows, kv),
            *reduce_space(rows, kv // 2, (2,)),
            *reduce_space(rank, wide),
            pltpu.VMEM((n_group, rank, wide), BF),
            pltpu.SemaphoreType.DMA((count,)),
            pltpu.SemaphoreType.DMA((count,)),
        ],
        compiler_params=pltpu.CompilerParams(
            collective_id=0, has_side_effects=True, vmem_limit_bytes=56 * 1024 * 1024
        ),
        name="value_backward",
    )(
        response_rows, prompt_rows, queries, cotangent, frozen_value_weight,
        response_keys, prompt_keys, segment_index, prompt_choice, value_adapter_down.T, value_adapter_up,
    )
    outs = pl.pallas_call(
        store,
        out_shape=tuple(jax.ShapeDtypeStruct(shape, kind) for shape, kind in shapes),
        in_specs=[vmem] * 6,
        out_specs=(pl.BlockSpec(memory_space=pltpu.HBM),) * 6,
        scratch_shapes=[pltpu.SemaphoreType.DMA((6,))],
        name="store",
    )(*outs)
    return (*outs[:4], outs[4].T, outs[5])


def solution(mesh):
    both = P(("group", "sample"), None)
    in_specs = (both,) * 8 + (P("sample", None), P("sample", None), P())
    out_specs = (both,) * 4 + (P("sample", None), P())
    return jax.shard_map(
        functools.partial(on_device, mesh.shape["group"], mesh.shape["sample"]),
        mesh=mesh, in_specs=in_specs, out_specs=out_specs, check_vma=False,
    )
```

```python
import functools

import jax
import jax.numpy as jnp
from jax import lax
from jax.experimental import pallas as pl
from jax.experimental.pallas import tpu as pltpu
from jax.sharding import PartitionSpec as P

HEADS = 32
KV_HEADS = 4
HEAD_DIM = 128
PROMPT_LEN = 128
GROUP_SIZE = HEADS // KV_HEADS
SCORE_SCALE = HEAD_DIM ** (-0.5)

adapter_scale = 2.0

BF = jnp.bfloat16
F32 = jnp.float32
MESH = pl.DeviceIdType.MESH


def nt(left, right):
    return lax.dot_general(left, right, (((1,), (1,)), ((), ())), preferred_element_type=F32)


def tn(left, right):
    return lax.dot_general(left, right, (((0,), (0,)), ((), ())), preferred_element_type=F32)


def nn(left, right):
    return lax.dot_general(left, right, (((1,), (0,)), ((), ())), preferred_element_type=F32)


class Slots:
    def __init__(self):
        self.count = 0

    def take(self, number):
        base = self.count
        self.count += number
        return base


def layout(nz, n_group):
    slots = Slots()
    places = {name: slots.take(nz) for name in (
        "k_z", "k_l", "k_c", "w_l", "d_z", "d_c", "v_z", "v_c",
        "w_z", "w_c", "w_x", "w_y", "w_d0", "w_d1",
        "rv_z", "rk_z", "rk_z2", "ra_z",
    )}
    for name in ("rv_c", "rk_c", "rk_c2", "ra_c"):
        places[name] = slots.take(1)
    places["g"] = slots.take(n_group)
    places["local"] = slots.take(5)
    return places, slots.count


def kernel(
    nz, n_group, places, factor,
    xr, xp, q, ct, w, rk, pk, seg, ch, dn, up,
    o_rg, o_pg, o_rk, o_pk, o_f, o_s,
    xv, qv, cv, wfull, kall, vall, dall, pmask, obias, prob, vlow, vloc, vp, acc,
    gv, gv_p, gv_h, gv_r, gk, gk_p, gk_h, gk_r, ga, ga_p, ga_h, ga_r, gg,
    ssem, rsem,
):
    g = lax.axis_index("group")
    j = lax.axis_index("sample")
    z = j // 2
    c = j % 2
    oc = 1 - c
    tokens = q.shape[0]
    rows = pk.shape[0]
    shard = w.shape[0]
    quarter = shard // 4
    half = quarter // 2
    prompts = 2 * nz * rows // PROMPT_LEN
    nzp = PROMPT_LEN // rows // 2
    partner = (g, j + 1 - 2 * c)
    gx = g + 1 - 2 * (g % 2)
    gy = g + 2 - 4 * ((g // 2) % 2)
    qme, qx, qy = g % 4, gx % 4, gy % 4
    qd = 3 - qme

    def zat(dz):
        return lax.rem(z + dz, nz)

    def zdev(dz):
        return (g, 2 * zat(dz) + c)

    def rcopy(src, dst, name, send, recv, device, recv_name=None):
        return pltpu.make_async_remote_copy(
            src_ref=src, dst_ref=dst,
            send_sem=ssem.at[places[name] + send], recv_sem=rsem.at[places[recv_name or name] + recv],
            device_id=device, device_id_type=MESH,
        )

    short = jnp.minimum(z, nz - 1 - z)

    def source(k):
        alternate = z + (k + 1) // 2 if k % 2 else z - k // 2
        one_side = jnp.where(2 * z < nz - 1, z + k - short, z - k + short)
        return jnp.where(k <= 2 * short, alternate, one_side)

    sources = [source(k) for k in range(1, nz)]

    sends = []

    def go(copy):
        copy.start()
        sends.append(copy)

    waits = []

    def go_if(condition, make):
        @pl.when(condition)
        def _():
            make().start()

        waits.append((condition, make))

    def chain_start(src, dst, name, name_left):
        go_if(z + 1 < nz, lambda: rcopy(src, dst, name, z, z, (g, jnp.minimum(j + 2, 2 * nz - 1))))
        go_if(z >= 1, lambda: rcopy(src, dst, name_left, z, z, (g, jnp.maximum(j - 2, 0)), name))

    def chain_next(there, name, src):
        rcopy(there, there, name, src, src, partner).wait_recv()
        after = jnp.where(src < z, z + 1, z - 1)
        inside = jnp.minimum(jnp.maximum(after, 0), nz - 1)
        go_if(after == inside, lambda: rcopy(there, there, name, src, src, (g, 2 * inside + c)))

    def gather_start(src, buf, name_z, name_c):
        for dz in range(1, nz):
            go(rcopy(src, buf.at[z, c], name_z, dz, nz - dz, zdev(dz)))
        go(rcopy(src, buf.at[z, c], name_c, 0, 0, partner))

    def gather_forward(buf, name_z, name_c):
        for dz in range(1, nz):
            there = buf.at[zat(dz), c]
            rcopy(there, there, name_z, dz, dz, zdev(dz)).wait_recv()
            go(rcopy(there, there, name_c, dz, dz, partner))

    def gather_finish(buf, name_c):
        for dz in range(nz):
            there = buf.at[zat(dz), oc]
            rcopy(there, there, name_c, dz, dz, partner).wait_recv()

    def scatter_pair(part, pair, name_c):
        go(rcopy(part.at[:, oc], pair, name_c, 0, 0, partner))

    def scatter_z(part, pair, held, slots, name_c, name_z):
        rcopy(part.at[:, oc], pair, name_c, 0, 0, partner).wait_recv()
        held[...] = (part[:, c].astype(F32) + pair[...].astype(F32)).astype(BF)
        for dz in range(1, nz):
            go(rcopy(held.at[zat(dz)], slots.at[z], name_z, dz, nz - dz, zdev(dz)))
        slots[z] = held[z]

    def scatter_sum(slots, name_z):
        for dz in range(1, nz):
            there = slots.at[zat(dz)]
            rcopy(there, there, name_z, dz, dz, zdev(dz)).wait_recv()
        total = slots[0].astype(F32)
        for at in range(1, nz):
            total = total + slots[at].astype(F32)
        return total

    local = [
        pltpu.make_async_copy(src, dst, ssem.at[places["local"] + at])
        for at, (src, dst) in enumerate((
            (q, qv), (ct, cv), (xr, xv.at[pl.ds(0, tokens)]), (xp, xv.at[pl.ds(tokens, rows)])))
    ]
    for copy in local:
        copy.start()

    barrier = pltpu.get_barrier_semaphore()
    for dz in range(1, nz):
        pl.semaphore_signal(barrier, inc=1, device_id=zdev(dz), device_id_type=MESH)
    pl.semaphore_signal(barrier, inc=1, device_id=partner, device_id_type=MESH)
    for dg in range(1, n_group):
        pl.semaphore_signal(barrier, inc=1, device_id=(lax.rem(g + dg, n_group), j), device_id_type=MESH)
    pl.semaphore_wait(barrier, nz + n_group - 1)

    mine = pl.ds(pl.multiple_of(qme * quarter, 16), quarter)
    chain_start(pk, kall.at[z, c], "k_z", "k_l")
    go(rcopy(pk, kall.at[z, c], "k_c", z, z, partner))
    chain_start(w.at[mine], wfull.at[z, c, mine], "w_z", "w_l")
    go(rcopy(w, wfull.at[z, c], "w_c", z, z, partner))
    own_w = pltpu.make_async_copy(w, wfull.at[z, c], ssem.at[places["local"] + 4])
    own_w.start()

    dall[z, c] = dn[...]
    gather_start(dn, dall, "d_z", "d_c")
    kall[z, c] = pk[...]

    seg_row = jnp.broadcast_to(seg[...], (tokens, tokens)).astype(F32)
    seg_col = jnp.transpose(seg_row)
    token = lax.broadcasted_iota(jnp.int32, (tokens, tokens), 0)
    other = lax.broadcasted_iota(jnp.int32, (tokens, tokens), 1)
    obias[...] = jnp.where((seg_row == seg_col) & (token <= other), 0.0, -1e30)
    choice = jnp.zeros((tokens, tokens), jnp.int32)
    for at in range(ch.shape[1]):
        choice = jnp.where(seg_col == float(at), ch[0, at], choice)
    for at in range(prompts):
        pmask[at] = jnp.where(choice == at, 1.0, 0.0).astype(BF)

    def stack(ref, head):
        return [ref[:, pl.ds(pl.multiple_of((head * GROUP_SIZE + at) * HEAD_DIM, HEAD_DIM), HEAD_DIM)]
                for at in range(GROUP_SIZE)]

    def masked(parts):
        return jnp.concatenate(
            [jnp.concatenate([part * pmask[at] for part in parts], axis=0) for at in range(prompts)], axis=1)

    def side(buf, lanes):
        return jnp.concatenate(
            [buf[at * nzp:(at + 1) * nzp, :, :, lanes].reshape(PROMPT_LEN, HEAD_DIM) for at in range(prompts)],
            axis=1)

    def with_own(prompt_side, own):
        return jnp.concatenate([prompt_side, jnp.concatenate([own] * prompts, axis=1)], axis=0)

    def own_sum(grads):
        total = grads[PROMPT_LEN:, 0:HEAD_DIM]
        for at in range(1, prompts):
            total = total + grads[PROMPT_LEN:, at * HEAD_DIM:(at + 1) * HEAD_DIM]
        return total

    def head_lanes(head):
        return pl.ds(pl.multiple_of(head * HEAD_DIM, HEAD_DIM), HEAD_DIM)

    def spread(buf, lanes, block):
        for at in range(prompts):
            buf[at * nzp:(at + 1) * nzp, :, :, lanes] = block[
                :, at * HEAD_DIM:(at + 1) * HEAD_DIM].astype(BF).reshape(nzp, 2, rows, HEAD_DIM)

    def softmax_head(head):
        lanes = head_lanes(head)
        qs = stack(qv, head)
        scores = nt(with_own(side(kall, lanes), rk[:, lanes]), masked(qs)) * SCORE_SCALE
        s_sel = scores[:PROMPT_LEN]
        s_own = scores[PROMPT_LEN:] + jnp.concatenate([obias[...]] * GROUP_SIZE, axis=1)
        top = jnp.max(jnp.maximum(s_sel, s_own), axis=0, keepdims=True)
        e_sel = jnp.exp(s_sel - top)
        e_own = jnp.exp(s_own - top)
        inv = 1.0 / jnp.sum(e_sel + e_own, axis=0, keepdims=True)
        p_sel = e_sel * inv
        p_own = e_own * inv
        prob[head, 0:PROMPT_LEN] = p_sel
        prob[head, PROMPT_LEN:] = p_own
        cs = stack(cv, head)
        grads = nn(jnp.concatenate([p_sel.astype(BF), p_own.astype(BF)], axis=0), masked(cs))
        spread(gv, lanes, grads[:PROMPT_LEN])
        vlow[0:tokens, lanes] = own_sum(grads).astype(BF)

    def w_plane(src):
        there = wfull.at[src, c, mine]
        chain_next(there, "w_z", src)
        go(rcopy(there, there, "w_x", src, src, (gx, j)))
        go(rcopy(there, there, "w_y", src, src, (gy, j)))

    def w_diagonal(src):
        there = wfull.at[src, c, pl.ds(pl.multiple_of(qx * quarter, 16), quarter)]
        rcopy(there, there, "w_x", src, src, (gx, j)).wait_recv()
        first = wfull.at[src, c, pl.ds(pl.multiple_of(qx * quarter, 16), half)]
        go(rcopy(first, first, "w_d0", src, src, (gy, j)))
        there = wfull.at[src, c, pl.ds(pl.multiple_of(qy * quarter, 16), quarter)]
        rcopy(there, there, "w_y", src, src, (gy, j)).wait_recv()
        second = wfull.at[src, c, pl.ds(pl.multiple_of(qy * quarter + half, 16), half)]
        go(rcopy(second, second, "w_d1", src, src, (gx, j)))

    def w_chip(src):
        first = wfull.at[src, c, pl.ds(pl.multiple_of(qd * quarter, 16), half)]
        rcopy(first, first, "w_d0", src, src, (gy, j)).wait_recv()
        second = wfull.at[src, c, pl.ds(pl.multiple_of(qd * quarter + half, 16), half)]
        rcopy(second, second, "w_d1", src, src, (gx, j)).wait_recv()
        there = wfull.at[src, c]
        go(rcopy(there, there, "w_c", src, src, partner))

    for src in sources:
        there = kall.at[src, c]
        chain_next(there, "k_z", src)
        go(rcopy(there, there, "k_c", src, src, partner))
    local[0].wait()
    local[1].wait()
    for at in range(nz):
        there = kall.at[at, oc]
        rcopy(there, there, "k_c", at, at, partner).wait_recv()

    last = nz - 2
    for head in range(KV_HEADS):
        for at in range(nz - 1):
            if min(at, KV_HEADS - 1) == head:
                w_plane(sources[at])
        for at in range(last):
            if min(at + 1, KV_HEADS - 1) == head:
                w_diagonal(sources[at])
        softmax_head(head)
    scatter_pair(gv, gv_p, "rv_c")
    w_diagonal(sources[last])
    for at in range(last):
        w_chip(sources[at])
    gather_forward(dall, "d_z", "d_c")
    scatter_z(gv, gv_p, gv_h, gv_r, "rv_c", "rv_z")
    gather_finish(dall, "d_c")
    local[2].wait()
    local[3].wait()
    own_w.wait()

    def columns(z_at, c_at):
        return pl.ds(pl.multiple_of((2 * z_at + c_at) * shard, 128), shard)

    def low_part(z_at, c_at):
        return nt(xv[:, columns(z_at, c_at)], dall[z_at, c_at])

    def low_step(at, carry):
        return carry + low_part(at // 2, at % 2)

    first_proj = lax.fori_loop(1, 2 * nz, low_step, low_part(0, 0)).astype(BF)

    def forward(z_at, c_at, first):
        base = nn(xv[:, columns(z_at, c_at)], wfull[z_at, c_at])
        acc[...] = base if first else acc[...] + base

    forward(z, c, True)
    w_chip(sources[last])
    rcopy(wfull.at[z, oc], wfull.at[z, oc], "w_c", z, z, partner).wait_recv()
    forward(z, oc, False)
    for src in sources[:last]:
        forward(src, c, False)

    vlow[tokens:] = scatter_sum(gv_r, "rv_z").astype(BF)
    back_all = nt(vlow[...], up[...]).astype(BF)
    second = tn(first_proj, vlow[...]).astype(BF)

    def adapter(at, carry):
        z_at, c_at = at // 2, at % 2
        ga[z_at, c_at, :, 0:shard] = tn(back_all, xv[:, columns(z_at, c_at)]).astype(BF)
        ga[z_at, c_at, :, shard:] = second
        return carry

    lax.fori_loop(0, 2 * nz, adapter, 0)
    scatter_pair(ga, ga_p, "ra_c")

    forward(sources[last], c, False)
    for src in sources:
        there = wfull.at[src, oc]
        rcopy(there, there, "w_c", src, src, partner).wait_recv()
        forward(src, oc, False)
    values = (acc[...] + adapter_scale * nn(first_proj, up[...])).astype(BF)
    vp[...] = values[tokens:]
    vloc[...] = values[:tokens]
    vall[z, c] = values[tokens:]
    gather_start(vp, vall, "v_z", "v_c")

    def back(at, carry):
        z_at, c_at = at // 2, at % 2
        grad = (nt(vlow[...], wfull[z_at, c_at]) + adapter_scale * nn(back_all, dall[z_at, c_at])).astype(BF)
        o_rg[:, columns(z_at, c_at)] = grad[:tokens]
        o_pg[:, columns(z_at, c_at)] = grad[tokens:]
        return carry

    scatter_z(ga, ga_p, ga_h, ga_r, "ra_c", "ra_z")
    lax.fori_loop(0, nz, back, 0)
    gather_forward(vall, "v_z", "v_c")
    gg[g] = scatter_sum(ga_r, "ra_z").astype(BF)
    for dg in range(1, n_group):
        there = lax.rem(g + dg, n_group)
        go(rcopy(gg.at[g], gg.at[g], "g", dg, n_group - dg, (there, j)))
    gather_finish(vall, "v_c")

    def key_head(head, carry):
        lanes = head_lanes(head)
        cs = stack(cv, head)
        grad_full = nt(with_own(side(vall, lanes), vloc[:, lanes]), masked(cs))
        full = prob[head]
        delta = jnp.sum(full.astype(BF).astype(F32) * grad_full, axis=0, keepdims=True)
        grad_low = (full * (grad_full - delta)).astype(BF)
        qs = stack(qv, head)
        per_half = KV_HEADS // 2
        grads = nn(grad_low, masked(qs)) * SCORE_SCALE
        spread(gk.at[head // per_half], head_lanes(head % per_half), grads[:PROMPT_LEN])
        o_rk[:, lanes] = own_sum(grads).astype(BF)
        return carry

    lax.fori_loop(0, KV_HEADS // 2, key_head, 0)
    scatter_pair(gk.at[0], gk_p.at[0], "rk_c")
    lax.fori_loop(KV_HEADS // 2, KV_HEADS - 1, key_head, 0)
    scatter_z(gk.at[0], gk_p.at[0], gk_h.at[0], gk_r.at[0], "rk_c", "rk_z")
    lax.fori_loop(KV_HEADS - 1, KV_HEADS, key_head, 0)
    scatter_pair(gk.at[1], gk_p.at[1], "rk_c2")
    scatter_z(gk.at[1], gk_p.at[1], gk_h.at[1], gk_r.at[1], "rk_c2", "rk_z2")
    lax.fori_loop(nz, 2 * nz, back, 0)
    for dg in range(1, n_group):
        there = lax.rem(g + dg, n_group)
        rcopy(gg.at[there], gg.at[there], "g", dg, dg, (there, j)).wait_recv()
    total = gg[0].astype(F32)
    for at in range(1, n_group):
        total = total + gg[at].astype(F32)
    total = total * factor
    o_f[...] = total[:, 0:shard]
    o_s[...] = total[:, shard:]
    width = o_pk.shape[1] // 2
    o_pk[:, 0:width] = scatter_sum(gk_r.at[0], "rk_z").astype(BF)
    o_pk[:, width:] = scatter_sum(gk_r.at[1], "rk_z2").astype(BF)
    for copy in sends:
        copy.wait_send()
    for condition, make in waits:
        @pl.when(condition)
        def _():
            make().wait_send()


def store(*refs):
    sem = refs[12]
    copies = [pltpu.make_async_copy(refs[at], refs[6 + at], sem.at[at]) for at in range(6)]
    for copy in copies:
        copy.start()
    for copy in copies:
        copy.wait()


def on_device(
    n_group, n_sample,
    response_rows, prompt_rows, queries, response_keys, prompt_keys, cotangent,
    segment_index, prompt_choice, frozen_value_weight, value_adapter_down, value_adapter_up,
):
    tokens, d = response_rows.shape
    rows, kv = prompt_keys.shape
    shard, rank = value_adapter_down.shape
    nz = n_sample // 2
    places, count = layout(nz, n_group)
    factor = adapter_scale * float((tokens + rows) * n_group * n_sample) ** (-0.5)
    wide = shard + kv
    any_space = pl.BlockSpec(memory_space=pl.ANY)
    vmem = pl.BlockSpec(memory_space=pltpu.VMEM)
    smem = pl.BlockSpec(memory_space=pltpu.SMEM)

    def reduce_space(high, across, lead=()):
        return [
            pltpu.VMEM((*lead, nz, 2, high, across), BF),
            pltpu.VMEM((*lead, nz, high, across), BF),
            pltpu.VMEM((*lead, nz, high, across), BF),
            pltpu.VMEM((*lead, nz, high, across), BF),
        ]

    shapes = (
        ((tokens, d), BF), ((rows, d), BF), ((tokens, kv), BF), ((rows, kv), BF),
        ((rank, shard), F32), ((rank, kv), F32),
    )
    outs = pl.pallas_call(
        functools.partial(kernel, nz, n_group, places, factor),
        out_shape=tuple(jax.ShapeDtypeStruct(shape, kind) for shape, kind in shapes),
        in_specs=[any_space] * 5 + [vmem] * 3 + [smem] + [vmem] * 2,
        out_specs=(vmem,) * 6,
        scratch_shapes=[
            pltpu.VMEM((tokens + rows, d), BF),
            pltpu.VMEM((tokens, HEADS * HEAD_DIM), BF),
            pltpu.VMEM((tokens, HEADS * HEAD_DIM), BF),
            pltpu.VMEM((nz, 2, shard, kv), BF),
            pltpu.VMEM((nz, 2, rows, kv), BF),
            pltpu.VMEM((nz, 2, rows, kv), BF),
            pltpu.VMEM((nz, 2, rank, shard), BF),
            pltpu.VMEM((n_sample * rows // PROMPT_LEN, tokens, HEAD_DIM), BF),
            pltpu.VMEM((tokens, tokens), F32),
            pltpu.VMEM((KV_HEADS, PROMPT_LEN + tokens, GROUP_SIZE * tokens), F32),
            pltpu.VMEM((tokens + rows, kv), BF),
            pltpu.VMEM((tokens, kv), BF),
            pltpu.VMEM((rows, kv), BF),
            pltpu.VMEM((tokens + rows, kv), F32),
            *reduce_space(rows, kv),
            *reduce_space(rows, kv // 2, (2,)),
            *reduce_space(rank, wide),
            pltpu.VMEM((n_group, rank, wide), BF),
            pltpu.SemaphoreType.DMA((count,)),
            pltpu.SemaphoreType.DMA((count,)),
        ],
        compiler_params=pltpu.CompilerParams(
            collective_id=0, has_side_effects=True, vmem_limit_bytes=56 * 1024 * 1024
        ),
        name="value_backward",
    )(
        response_rows, prompt_rows, queries, cotangent, frozen_value_weight,
        response_keys, prompt_keys, segment_index, prompt_choice, value_adapter_down.T, value_adapter_up,
    )
    outs = pl.pallas_call(
        store,
        out_shape=tuple(jax.ShapeDtypeStruct(shape, kind) for shape, kind in shapes),
        in_specs=[vmem] * 6,
        out_specs=(pl.BlockSpec(memory_space=pltpu.HBM),) * 6,
        scratch_shapes=[pltpu.SemaphoreType.DMA((6,))],
        name="store",
    )(*outs)
    return (*outs[:4], outs[4].T, outs[5])


def solution(mesh):
    both = P(("group", "sample"), None)
    in_specs = (both,) * 8 + (P("sample", None), P("sample", None), P())
    out_specs = (both,) * 4 + (P("sample", None), P())
    return jax.shard_map(
        functools.partial(on_device, mesh.shape["group"], mesh.shape["sample"]),
        mesh=mesh, in_specs=in_specs, out_specs=out_specs, check_vma=False,
    )
```

```python
import functools

import jax
import jax.numpy as jnp
from jax import lax
from jax.experimental import pallas as pl
from jax.experimental.pallas import tpu as pltpu
from jax.sharding import PartitionSpec as P

HEADS = 32
KV_HEADS = 4
HEAD_DIM = 128
PROMPT_LEN = 128
GROUP_SIZE = HEADS // KV_HEADS
SCORE_SCALE = HEAD_DIM ** (-0.5)

adapter_scale = 2.0

BF = jnp.bfloat16
F32 = jnp.float32
MESH = pl.DeviceIdType.MESH


def nt(left, right):
    return lax.dot_general(left, right, (((1,), (1,)), ((), ())), preferred_element_type=F32)


def tn(left, right):
    return lax.dot_general(left, right, (((0,), (0,)), ((), ())), preferred_element_type=F32)


def nn(left, right):
    return lax.dot_general(left, right, (((1,), (0,)), ((), ())), preferred_element_type=F32)


class Slots:
    def __init__(self):
        self.count = 0

    def take(self, number):
        base = self.count
        self.count += number
        return base


def layout(nz, n_group):
    slots = Slots()
    places = {name: slots.take(nz) for name in (
        "k_z", "k_l", "k_c", "w_l", "d_z", "d_c", "v_z", "v_c",
        "w_z", "w_c", "w_x", "w_y", "w_d0", "w_d1",
        "rv_z", "rk_z", "rk_z2", "ra_z",
    )}
    for name in ("rv_c", "rk_c", "rk_c2", "ra_c"):
        places[name] = slots.take(1)
    places["g"] = slots.take(n_group)
    places["local"] = slots.take(5)
    return places, slots.count


def kernel(
    nz, n_group, places, factor,
    xr, xp, q, ct, w, rk, pk, seg, ch, dn, up,
    o_rg, o_pg, o_rk, o_pk, o_f, o_s,
    xv, qv, cv, wfull, kall, vall, dall, pmask, tmask, obias, prob, vlow, vloc, vp, acc, low,
    gv, gv_p, gv_h, gv_r, gk, gk_p, gk_h, gk_r, ga, ga_p, ga_h, ga_r, gg,
    ssem, rsem,
):
    g = lax.axis_index("group")
    j = lax.axis_index("sample")
    z = j // 2
    c = j % 2
    oc = 1 - c
    tokens = q.shape[0]
    rows = pk.shape[0]
    shard = w.shape[0]
    quarter = shard // 4
    half = quarter // 2
    prompts = 2 * nz * rows // PROMPT_LEN
    nzp = PROMPT_LEN // rows // 2
    partner = (g, j + 1 - 2 * c)
    gx = g + 1 - 2 * (g % 2)
    gy = g + 2 - 4 * ((g // 2) % 2)
    qme, qx, qy = g % 4, gx % 4, gy % 4
    qd = 3 - qme

    def zat(dz):
        return lax.rem(z + dz, nz)

    def zdev(dz):
        return (g, 2 * zat(dz) + c)

    def rcopy(src, dst, name, send, recv, device, recv_name=None):
        return pltpu.make_async_remote_copy(
            src_ref=src, dst_ref=dst,
            send_sem=ssem.at[places[name] + send], recv_sem=rsem.at[places[recv_name or name] + recv],
            device_id=device, device_id_type=MESH,
        )

    short = jnp.minimum(z, nz - 1 - z)

    def source(k):
        alternate = z + (k + 1) // 2 if k % 2 else z - k // 2
        one_side = jnp.where(2 * z < nz - 1, z + k - short, z - k + short)
        return jnp.where(k <= 2 * short, alternate, one_side)

    sources = [source(k) for k in range(1, nz)]

    sends = []

    def go(copy):
        copy.start()
        sends.append(copy)

    waits = []

    def go_if(condition, make):
        @pl.when(condition)
        def _():
            make().start()

        waits.append((condition, make))

    def chain_start(src, dst, name, name_left):
        go_if(z + 1 < nz, lambda: rcopy(src, dst, name, z, z, (g, jnp.minimum(j + 2, 2 * nz - 1))))
        go_if(z >= 1, lambda: rcopy(src, dst, name_left, z, z, (g, jnp.maximum(j - 2, 0)), name))

    def chain_next(there, name, src):
        rcopy(there, there, name, src, src, partner).wait_recv()
        after = jnp.where(src < z, z + 1, z - 1)
        inside = jnp.minimum(jnp.maximum(after, 0), nz - 1)
        go_if(after == inside, lambda: rcopy(there, there, name, src, src, (g, 2 * inside + c)))

    def gather_start(src, buf, name_z, name_c):
        for dz in range(1, nz):
            go(rcopy(src, buf.at[z, c], name_z, dz, nz - dz, zdev(dz)))
        go(rcopy(src, buf.at[z, c], name_c, 0, 0, partner))

    def gather_forward(buf, name_z, name_c):
        for dz in range(1, nz):
            there = buf.at[zat(dz), c]
            rcopy(there, there, name_z, dz, dz, zdev(dz)).wait_recv()
            go(rcopy(there, there, name_c, dz, dz, partner))

    def gather_finish(buf, name_c):
        for dz in range(nz):
            there = buf.at[zat(dz), oc]
            rcopy(there, there, name_c, dz, dz, partner).wait_recv()

    def scatter_pair(part, pair, name_c):
        go(rcopy(part.at[:, oc], pair, name_c, 0, 0, partner))

    def scatter_z(part, pair, held, slots, name_c, name_z):
        rcopy(part.at[:, oc], pair, name_c, 0, 0, partner).wait_recv()
        held[...] = (part[:, c].astype(F32) + pair[...].astype(F32)).astype(BF)
        for dz in range(1, nz):
            go(rcopy(held.at[zat(dz)], slots.at[z], name_z, dz, nz - dz, zdev(dz)))
        slots[z] = held[z]

    def scatter_sum(slots, name_z):
        for dz in range(1, nz):
            there = slots.at[zat(dz)]
            rcopy(there, there, name_z, dz, dz, zdev(dz)).wait_recv()
        total = slots[0].astype(F32)
        for at in range(1, nz):
            total = total + slots[at].astype(F32)
        return total

    local = [
        pltpu.make_async_copy(src, dst, ssem.at[places["local"] + at])
        for at, (src, dst) in enumerate((
            (q, qv), (ct, cv), (xr, xv.at[pl.ds(0, tokens)]), (xp, xv.at[pl.ds(tokens, rows)])))
    ]
    for copy in local:
        copy.start()

    barrier = pltpu.get_barrier_semaphore()
    for dz in range(1, nz):
        pl.semaphore_signal(barrier, inc=1, device_id=zdev(dz), device_id_type=MESH)
    pl.semaphore_signal(barrier, inc=1, device_id=partner, device_id_type=MESH)
    for dg in range(1, n_group):
        pl.semaphore_signal(barrier, inc=1, device_id=(lax.rem(g + dg, n_group), j), device_id_type=MESH)
    pl.semaphore_wait(barrier, nz + n_group - 1)

    mine = pl.ds(pl.multiple_of(qme * quarter, 16), quarter)
    chain_start(pk, kall.at[z, c], "k_z", "k_l")
    go(rcopy(pk, kall.at[z, c], "k_c", z, z, partner))
    chain_start(w.at[mine], wfull.at[z, c, mine], "w_z", "w_l")
    go(rcopy(w, wfull.at[z, c], "w_c", z, z, partner))
    own_w = pltpu.make_async_copy(w, wfull.at[z, c], ssem.at[places["local"] + 4])
    own_w.start()

    dall[z, c] = dn[...]
    gather_start(dn, dall, "d_z", "d_c")
    kall[z, c] = pk[...]

    seg_row = jnp.broadcast_to(seg[...], (tokens, tokens)).astype(F32)
    seg_col = jnp.transpose(seg_row)
    token = lax.broadcasted_iota(jnp.int32, (tokens, tokens), 0)
    other = lax.broadcasted_iota(jnp.int32, (tokens, tokens), 1)
    obias[...] = jnp.where((seg_row == seg_col) & (token <= other), 0.0, -1e30)
    for mask, segment in ((pmask, seg_col), (tmask, seg_row)):
        choice = jnp.zeros((tokens, tokens), jnp.int32)
        for at in range(ch.shape[1]):
            choice = jnp.where(segment == float(at), ch[0, at], choice)
        for at in range(prompts):
            mask[at] = jnp.where(choice == at, 1.0, 0.0).astype(BF)

    def stack(ref, head):
        return [ref[:, pl.ds(pl.multiple_of((head * GROUP_SIZE + at) * HEAD_DIM, HEAD_DIM), HEAD_DIM)]
                for at in range(GROUP_SIZE)]

    def masked(parts):
        return jnp.concatenate(
            [jnp.concatenate([part * pmask[at] for part in parts], axis=0) for at in range(prompts)], axis=1)

    def side(buf, lanes):
        return jnp.concatenate(
            [buf[at * nzp:(at + 1) * nzp, :, :, lanes].reshape(PROMPT_LEN, HEAD_DIM) for at in range(prompts)],
            axis=1)

    def masked_turned(parts):
        turned = [jnp.transpose(part) for part in parts]
        return jnp.concatenate(
            [jnp.concatenate([part * tmask[at] for part in turned], axis=1) for at in range(prompts)], axis=0)

    def with_own(prompt_side, own):
        return jnp.concatenate([prompt_side, jnp.concatenate([own] * prompts, axis=1)], axis=0)

    def own_sum(grads):
        total = grads[PROMPT_LEN:, 0:HEAD_DIM]
        for at in range(1, prompts):
            total = total + grads[PROMPT_LEN:, at * HEAD_DIM:(at + 1) * HEAD_DIM]
        return total

    def head_lanes(head):
        return pl.ds(pl.multiple_of(head * HEAD_DIM, HEAD_DIM), HEAD_DIM)

    def spread(buf, lanes, block):
        for at in range(prompts):
            buf[at * nzp:(at + 1) * nzp, :, :, lanes] = block[
                :, at * HEAD_DIM:(at + 1) * HEAD_DIM].astype(BF).reshape(nzp, 2, rows, HEAD_DIM)

    def softmax_head(head):
        lanes = head_lanes(head)
        qs = stack(qv, head)
        scores = nn(with_own(side(kall, lanes), rk[:, lanes]), masked_turned(qs)) * SCORE_SCALE
        s_sel = scores[:PROMPT_LEN]
        s_own = scores[PROMPT_LEN:] + jnp.concatenate([obias[...]] * GROUP_SIZE, axis=1)
        top = jnp.max(jnp.maximum(s_sel, s_own), axis=0, keepdims=True)
        e_sel = jnp.exp(s_sel - top)
        e_own = jnp.exp(s_own - top)
        inv = 1.0 / jnp.sum(e_sel + e_own, axis=0, keepdims=True)
        p_sel = e_sel * inv
        p_own = e_own * inv
        prob[head, 0:PROMPT_LEN] = p_sel
        prob[head, PROMPT_LEN:] = p_own
        cs = stack(cv, head)
        grads = nn(jnp.concatenate([p_sel.astype(BF), p_own.astype(BF)], axis=0), masked(cs))
        spread(gv, lanes, grads[:PROMPT_LEN])
        vlow[0:tokens, lanes] = own_sum(grads).astype(BF)

    def w_plane(src):
        there = wfull.at[src, c, mine]
        chain_next(there, "w_z", src)
        go(rcopy(there, there, "w_x", src, src, (gx, j)))
        go(rcopy(there, there, "w_y", src, src, (gy, j)))

    def w_diagonal(src):
        there = wfull.at[src, c, pl.ds(pl.multiple_of(qx * quarter, 16), quarter)]
        rcopy(there, there, "w_x", src, src, (gx, j)).wait_recv()
        first = wfull.at[src, c, pl.ds(pl.multiple_of(qx * quarter, 16), half)]
        go(rcopy(first, first, "w_d0", src, src, (gy, j)))
        there = wfull.at[src, c, pl.ds(pl.multiple_of(qy * quarter, 16), quarter)]
        rcopy(there, there, "w_y", src, src, (gy, j)).wait_recv()
        second = wfull.at[src, c, pl.ds(pl.multiple_of(qy * quarter + half, 16), half)]
        go(rcopy(second, second, "w_d1", src, src, (gx, j)))

    def w_chip(src):
        first = wfull.at[src, c, pl.ds(pl.multiple_of(qd * quarter, 16), half)]
        rcopy(first, first, "w_d0", src, src, (gy, j)).wait_recv()
        second = wfull.at[src, c, pl.ds(pl.multiple_of(qd * quarter + half, 16), half)]
        rcopy(second, second, "w_d1", src, src, (gx, j)).wait_recv()
        there = wfull.at[src, c]
        go(rcopy(there, there, "w_c", src, src, partner))

    for src in sources:
        there = kall.at[src, c]
        chain_next(there, "k_z", src)
        go(rcopy(there, there, "k_c", src, src, partner))
    local[0].wait()
    local[1].wait()
    for at in range(nz):
        there = kall.at[at, oc]
        rcopy(there, there, "k_c", at, at, partner).wait_recv()

    stages = []
    for at in range(nz + 1):
        if at < nz - 1:
            stages.append(functools.partial(w_plane, sources[at]))
        if 0 <= at - 1 < nz - 1:
            stages.append(functools.partial(w_diagonal, sources[at - 1]))
        if 0 <= at - 2 < nz - 1:
            stages.append(functools.partial(w_chip, sources[at - 2]))
    per_head = -(-len(stages) // (KV_HEADS + 1))
    for head in range(KV_HEADS):
        for stage in stages[head * per_head:(head + 1) * per_head]:
            stage()
        softmax_head(head)
    scatter_pair(gv, gv_p, "rv_c")
    for stage in stages[KV_HEADS * per_head:]:
        stage()
    gather_forward(dall, "d_z", "d_c")
    scatter_z(gv, gv_p, gv_h, gv_r, "rv_c", "rv_z")
    gather_finish(dall, "d_c")
    local[2].wait()
    local[3].wait()
    own_w.wait()

    def columns(z_at, c_at):
        return pl.ds(pl.multiple_of((2 * z_at + c_at) * shard, 128), shard)

    def forward(z_at, c_at, first):
        x = xv[:, columns(z_at, c_at)]
        base = nn(x, wfull[z_at, c_at])
        lowest = nt(x, dall[z_at, c_at])
        acc[...] = base if first else acc[...] + base
        low[...] = lowest if first else low[...] + lowest

    forward(z, c, True)
    for src in sources:
        forward(src, c, False)
    for src in [z] + sources:
        there = wfull.at[src, oc]
        rcopy(there, there, "w_c", src, src, partner).wait_recv()
        forward(src, oc, False)
    first_proj = low[...].astype(BF)
    values = (acc[...] + adapter_scale * nn(first_proj, up[...])).astype(BF)
    vp[...] = values[tokens:]
    vloc[...] = values[:tokens]
    vall[z, c] = values[tokens:]
    gather_start(vp, vall, "v_z", "v_c")

    vlow[tokens:] = scatter_sum(gv_r, "rv_z").astype(BF)
    back_all = nt(vlow[...], up[...]).astype(BF)
    second = tn(first_proj, vlow[...]).astype(BF)

    def adapter(at, carry):
        z_at, c_at = at // 2, at % 2
        ga[z_at, c_at, :, 0:shard] = tn(back_all, xv[:, columns(z_at, c_at)]).astype(BF)
        ga[z_at, c_at, :, shard:] = second
        return carry

    lax.fori_loop(0, 2 * nz, adapter, 0)
    scatter_pair(ga, ga_p, "ra_c")

    def back(at, carry):
        z_at, c_at = at // 2, at % 2
        grad = (nt(vlow[...], wfull[z_at, c_at]) + adapter_scale * nn(back_all, dall[z_at, c_at])).astype(BF)
        o_rg[:, columns(z_at, c_at)] = grad[:tokens]
        o_pg[:, columns(z_at, c_at)] = grad[tokens:]
        return carry

    lax.fori_loop(0, nz, back, 0)
    gather_forward(vall, "v_z", "v_c")
    scatter_z(ga, ga_p, ga_h, ga_r, "ra_c", "ra_z")
    gather_finish(vall, "v_c")

    def key_head(head, carry):
        lanes = head_lanes(head)
        cs = stack(cv, head)
        grad_full = nn(with_own(side(vall, lanes), vloc[:, lanes]), masked_turned(cs))
        full = prob[head]
        delta = jnp.sum(full.astype(BF).astype(F32) * grad_full, axis=0, keepdims=True)
        grad_low = (full * (grad_full - delta)).astype(BF)
        qs = stack(qv, head)
        per_half = KV_HEADS // 2
        grads = nn(grad_low, masked(qs)) * SCORE_SCALE
        spread(gk.at[head // per_half], head_lanes(head % per_half), grads[:PROMPT_LEN])
        o_rk[:, lanes] = own_sum(grads).astype(BF)
        return carry

    lax.fori_loop(0, KV_HEADS // 2, key_head, 0)
    scatter_pair(gk.at[0], gk_p.at[0], "rk_c")
    lax.fori_loop(KV_HEADS // 2, KV_HEADS - 1, key_head, 0)
    scatter_z(gk.at[0], gk_p.at[0], gk_h.at[0], gk_r.at[0], "rk_c", "rk_z")
    gg[g] = scatter_sum(ga_r, "ra_z").astype(BF)
    for dg in range(1, n_group):
        there = lax.rem(g + dg, n_group)
        go(rcopy(gg.at[g], gg.at[g], "g", dg, n_group - dg, (there, j)))
    lax.fori_loop(KV_HEADS - 1, KV_HEADS, key_head, 0)
    scatter_pair(gk.at[1], gk_p.at[1], "rk_c2")
    scatter_z(gk.at[1], gk_p.at[1], gk_h.at[1], gk_r.at[1], "rk_c2", "rk_z2")
    lax.fori_loop(nz, 2 * nz, back, 0)
    for dg in range(1, n_group):
        there = lax.rem(g + dg, n_group)
        rcopy(gg.at[there], gg.at[there], "g", dg, dg, (there, j)).wait_recv()
    total = gg[0].astype(F32)
    for at in range(1, n_group):
        total = total + gg[at].astype(F32)
    total = total * factor
    o_f[...] = total[:, 0:shard]
    o_s[...] = total[:, shard:]
    width = o_pk.shape[1] // 2
    o_pk[:, 0:width] = scatter_sum(gk_r.at[0], "rk_z").astype(BF)
    o_pk[:, width:] = scatter_sum(gk_r.at[1], "rk_z2").astype(BF)
    for copy in sends:
        copy.wait_send()
    for condition, make in waits:
        @pl.when(condition)
        def _():
            make().wait_send()


def store(*refs):
    sem = refs[12]
    copies = [pltpu.make_async_copy(refs[at], refs[6 + at], sem.at[at]) for at in range(6)]
    for copy in copies:
        copy.start()
    for copy in copies:
        copy.wait()


def on_device(
    n_group, n_sample,
    response_rows, prompt_rows, queries, response_keys, prompt_keys, cotangent,
    segment_index, prompt_choice, frozen_value_weight, value_adapter_down, value_adapter_up,
):
    tokens, d = response_rows.shape
    rows, kv = prompt_keys.shape
    shard, rank = value_adapter_down.shape
    nz = n_sample // 2
    places, count = layout(nz, n_group)
    factor = adapter_scale * float((tokens + rows) * n_group * n_sample) ** (-0.5)
    wide = shard + kv
    any_space = pl.BlockSpec(memory_space=pl.ANY)
    vmem = pl.BlockSpec(memory_space=pltpu.VMEM)
    smem = pl.BlockSpec(memory_space=pltpu.SMEM)

    def reduce_space(high, across, lead=()):
        return [
            pltpu.VMEM((*lead, nz, 2, high, across), BF),
            pltpu.VMEM((*lead, nz, high, across), BF),
            pltpu.VMEM((*lead, nz, high, across), BF),
            pltpu.VMEM((*lead, nz, high, across), BF),
        ]

    shapes = (
        ((tokens, d), BF), ((rows, d), BF), ((tokens, kv), BF), ((rows, kv), BF),
        ((rank, shard), F32), ((rank, kv), F32),
    )
    outs = pl.pallas_call(
        functools.partial(kernel, nz, n_group, places, factor),
        out_shape=tuple(jax.ShapeDtypeStruct(shape, kind) for shape, kind in shapes),
        in_specs=[any_space] * 5 + [vmem] * 3 + [smem] + [vmem] * 2,
        out_specs=(vmem,) * 6,
        scratch_shapes=[
            pltpu.VMEM((tokens + rows, d), BF),
            pltpu.VMEM((tokens, HEADS * HEAD_DIM), BF),
            pltpu.VMEM((tokens, HEADS * HEAD_DIM), BF),
            pltpu.VMEM((nz, 2, shard, kv), BF),
            pltpu.VMEM((nz, 2, rows, kv), BF),
            pltpu.VMEM((nz, 2, rows, kv), BF),
            pltpu.VMEM((nz, 2, rank, shard), BF),
            pltpu.VMEM((n_sample * rows // PROMPT_LEN, tokens, HEAD_DIM), BF),
            pltpu.VMEM((n_sample * rows // PROMPT_LEN, HEAD_DIM, tokens), BF),
            pltpu.VMEM((tokens, tokens), F32),
            pltpu.VMEM((KV_HEADS, PROMPT_LEN + tokens, GROUP_SIZE * tokens), F32),
            pltpu.VMEM((tokens + rows, kv), BF),
            pltpu.VMEM((tokens, kv), BF),
            pltpu.VMEM((rows, kv), BF),
            pltpu.VMEM((tokens + rows, kv), F32),
            pltpu.VMEM((tokens + rows, rank), F32),
            *reduce_space(rows, kv),
            *reduce_space(rows, kv // 2, (2,)),
            *reduce_space(rank, wide),
            pltpu.VMEM((n_group, rank, wide), BF),
            pltpu.SemaphoreType.DMA((count,)),
            pltpu.SemaphoreType.DMA((count,)),
        ],
        compiler_params=pltpu.CompilerParams(
            collective_id=0, has_side_effects=True, vmem_limit_bytes=56 * 1024 * 1024
        ),
        name="value_backward",
    )(
        response_rows, prompt_rows, queries, cotangent, frozen_value_weight,
        response_keys, prompt_keys, segment_index, prompt_choice, value_adapter_down.T, value_adapter_up,
    )
    outs = pl.pallas_call(
        store,
        out_shape=tuple(jax.ShapeDtypeStruct(shape, kind) for shape, kind in shapes),
        in_specs=[vmem] * 6,
        out_specs=(pl.BlockSpec(memory_space=pltpu.HBM),) * 6,
        scratch_shapes=[pltpu.SemaphoreType.DMA((6,))],
        name="store",
    )(*outs)
    return (*outs[:4], outs[4].T, outs[5])


def solution(mesh):
    both = P(("group", "sample"), None)
    in_specs = (both,) * 8 + (P("sample", None), P("sample", None), P())
    out_specs = (both,) * 4 + (P("sample", None), P())
    return jax.shard_map(
        functools.partial(on_device, mesh.shape["group"], mesh.shape["sample"]),
        mesh=mesh, in_specs=in_specs, out_specs=out_specs, check_vma=False,
    )
```
